32 devices in a mesh: row: 8 (over y, x, core), col: 4 (over z).
Axes of the slice: x: 2, y: 2, z: 4, core: 2. Of those that a mesh axis runs over, the one named last changes fastest.
Arguments:
- attn_context: bfloat16 [4096, 4096], P('row', 'col'), may hold values from -6 to 6
- residual: bfloat16 [4096, 2048], P('row', 'col'), may hold values from -8 to 8
- w_out: bfloat16 [4096, 2048], P('col'), may hold values from -0.09375 to 0.09375
- gain_post: bfloat16 [2048], replicated, may hold values from 0.5 to 1.5
- gain_input: bfloat16 [2048], replicated, may hold values from 0.5 to 1.5
- routes: int32 [4096, 8], P('row'), may hold values from 0 to 15, all different within a row; in each aligned block of 512 rows (0 to 511, 512 to 1023, ...) at most 512 rows name the same one
- router_scores: float32 [4096, 8], P('row'), may hold values from 0.02 to 1
- w_gate: bfloat16 [32, 2048, 384], P(('row', 'col')), may hold values from -0.125 to 0.125
- w_up: bfloat16 [32, 2048, 384], P(('row', 'col')), may hold values from -0.125 to 0.125
- w_down: bfloat16 [32, 384, 2048], P(('row', 'col')), may hold values from -0.21875 to 0.21875
- w_query: bfloat16 [2048, 4096], P(None, 'col'), may hold values from -1 to 1
- w_keyval: bfloat16 [2048, 1024], P(None, 'col'), may hold values from -1 to 1
- segment_ids: int32 [8, 504], P('row'), may hold values from 0 to 3, never falling along the last dimension, each value on 1 to 252 neighbouring positions
- cache_lengths: int32 [64], P('row'), may hold values from 1 to 1024, 32768 in all
- holders: int32 [64], P('row'), may hold values from 0 to 63, each once
- cache_keys: bfloat16 [64, 1024, 512], P('row', 'col'), may hold values from -12 to 12
- cache_values: bfloat16 [64, 1024, 512], P('row', 'col'), may hold values from -12 to 12
Outputs:
- hidden_out: bfloat16 [4096, 2048], P('row', 'col')
- new_cache: bfloat16 [4096, 1024], P('row', 'col')
- attention_out: bfloat16 [4096, 4096], P('row', 'col')
The draws below stay inside these ranges and needn't reach their ends.
Inputs may be any that keep to these rules, and one draw needn't show every extreme that they name: `routes`: in the 512 rows of one index of row, no expert is named by more than 512 rows, and in every draw some expert is named by exactly 512. `segment_ids`: each prompt has at most 252 rows and one has exactly that many. `cache_lengths`: the lengths sum to 32768 and the largest is 1024. `holders`: each cache entry belongs to exactly one decode row.
All inputs are finite; a program needn't handle non-finite values. No bound on the sum of `cache_lengths` on one device may be relied on, other than what follows from the above.
Results may differ from the reference program's by a relative error of at most 0.0175.
Values may be sent and summed in bfloat16 or wider, within the bound.
No kernel may reach another device: no remote copies, remote signals or barrier semaphores. Data moves between devices by JAX's collectives and lax.ppermute only.
A program may use at most 128 MiB of HBM per device.

```python
import math
import jax
import jax.numpy as jnp
import numpy as np
from jax import lax

D = 2048
FF = 768
TOP = 8
QH = 32
KVH = 4
HD = 128
TOK_DEV = 512
DEC_DEV = 8
LMAX = 1024
EXPERTS = 16
HALF = 384
CAP = 512
PRE_DEV = 504
TOKENS = 4096
CACHES = 64
N_ROW = 8


def draw_residual(key, part):
    noise_rows = jax.random.truncated_normal(jax.random.fold_in(key, 101), -6.0, 6.0, (TOKENS, D), jnp.float32)
    return noise_rows.astype(jnp.bfloat16)


def draw_w_query(key, part):
    weight_scale = D ** (-0.5)
    values = weight_scale * jax.random.truncated_normal(jax.random.fold_in(key, 102), -4.0, 4.0, (D, QH * HD), jnp.float32)
    return values.astype(jnp.bfloat16)


def draw_w_keyval(key, part):
    weight_scale = D ** (-0.5)
    values = weight_scale * jax.random.truncated_normal(jax.random.fold_in(key, 103), -4.0, 4.0, (D, 2 * KVH * HD), jnp.float32)
    return values.astype(jnp.bfloat16)


def draw_cache_keys(key, part):
    values = jax.random.truncated_normal(jax.random.fold_in(key, 104), -6.0, 6.0, (CACHES, LMAX, KVH * HD), jnp.float32)
    return values.astype(jnp.bfloat16)


def draw_cache_values(key, part):
    place = jnp.arange(LMAX).astype(jnp.float32) / LMAX
    channel_sign = jnp.where(jax.random.bernoulli(jax.random.fold_in(key, 211), 0.5, (KVH * HD,)), 1.0, -1.0).astype(jnp.float32)
    noise = jax.random.truncated_normal(jax.random.fold_in(key, 105), -3.0, 3.0, (CACHES, LMAX, KVH * HD), jnp.float32)
    rise = 1.0 + 2.0 * place
    drift = 1.5
    values = noise * rise[None, :, None] + drift * place[None, :, None] * channel_sign[None, None, :]
    return jnp.clip(values, -12.0, 12.0).astype(jnp.bfloat16)


def steps_of(rng, shape, split, smallest, high):
    gain, own = 1.0, jax.random.fold_in(rng, 6)
    for dim, blocks in split:
        draws = jnp.exp(jax.random.uniform(jax.random.fold_in(own, dim), (blocks,), jnp.float32, smallest / len(split), high / len(split)))
        gain = gain * jnp.repeat(draws, shape[dim] // blocks).reshape([-1 if axis == dim else 1 for axis in range(len(shape))])
    return gain


def length_profile(number_of, total, reach, slope):
    weights = [(1 << 20) // math.isqrt(standing ** slope) + 1 for standing in range(2, number_of + 1)]
    surplus, given = total - reach - (number_of - 1), [1] * (number_of - 1)
    while surplus > 0:
        movable = [i for i in range(number_of - 1) if given[i] < reach]
        whole, remaining = sum([weights[i] for i in movable]), surplus
        for i in movable:
            extra = min(reach - given[i], max(1, remaining * weights[i] // whole), surplus)
            given[i] = given[i] + extra
            surplus = surplus - extra
    return np.array([reach] + given)


def uneven_parts(stream_key, amount, total, bound, lean):
    if amount == 2:
        one = jax.random.randint(stream_key, (), max(1, total - bound), min(bound, total - 1) + 1)
        return jnp.stack([one, total - one])
    sizes = jnp.asarray(length_profile(amount, total, bound, lean), jnp.int32)
    couples = (amount - 1) // 2
    donor, taker = sizes[1:1 + 2 * couples:2], sizes[2:2 + 2 * couples:2]
    slack = jnp.minimum(donor - 1, bound - taker)
    passed = jax.random.randint(jax.random.fold_in(stream_key, 1), (couples,), 0, 1 << 20) % (slack + 1)
    sizes = sizes.at[1:1 + 2 * couples:2].set(donor - passed).at[2:2 + 2 * couples:2].set(taker + passed)
    return sizes[jax.random.permutation(jax.random.fold_in(stream_key, 2), amount)]


def assign_block(own_key, own, number, rows, count, top, reach, skew):
    ranking = jax.random.permutation(own_key, count)
    heavy_load, ordinary = load_shares(count, rows * top, reach, skew, True), load_shares(count, rows * top, reach, skew, False)
    places = jnp.arange(count)

    def named(sizes, rotation):
        used = int((sizes > 0).sum())
        fixed = max(1, used // 4)
        moved = fixed + (places - fixed + rotation * (used - fixed)) % max(1, count - fixed)
        return jnp.zeros((count,), jnp.int32).at[ranking[jnp.where(places < fixed, places, moved)]].set(jnp.asarray(sizes, jnp.int32))

    sizes = jnp.where(number % 4 == 0, named(heavy_load, number // 4), named(ordinary, number - number // 4 - 1))
    mixed = jax.random.permutation(jax.random.fold_in(own, 3), count)
    source_of, taker = mixed[0:count // 2 * 2:2], mixed[1:count // 2 * 2:2]
    slack = jnp.minimum(sizes[source_of] - 1, reach - sizes[taker]) // 2
    slack = jnp.where((source_of == ranking[0]) | (taker == ranking[0]) | (sizes[taker] == 0), 0, jnp.maximum(slack, 0))
    moved = jax.random.randint(jax.random.fold_in(own, 4), (count // 2,), 0, 1 << 20) % (slack + 1)
    sizes = sizes.at[source_of].add(-moved).at[taker].add(moved)
    labels = jnp.searchsorted(jnp.cumsum(sizes), jnp.arange(rows * top), side="right").astype(jnp.int32)
    table = labels.reshape(top, rows).T
    table = table[jax.random.permutation(jax.random.fold_in(own, 1), rows)]
    rotation = jax.random.randint(jax.random.fold_in(own, 2), (rows, 1), 0, top)
    return jnp.take_along_axis(table, (jnp.arange(top)[None, :] + rotation) % top, axis=1)


def load_shares(amount, total, reach, slope, full):
    weights = [(1 << 20) // math.isqrt(standing ** slope) + 1 for standing in range(1, amount + 1)]
    largest = reach if full else min(reach, max(-(-total // amount), total * weights[0] // sum(weights)))
    least = 1 if total - largest >= amount - 1 else 0
    given, rest = [largest] + [least] * (amount - 1), total - largest - least * (amount - 1)
    while rest > 0:
        free = [i for i in range(1, amount) if given[i] < largest] or [i for i in range(1, amount) if given[i] < reach]
        pool, left = sum([weights[i] for i in free]), rest
        for i in free:
            addition = min(reach - given[i], max(1, left * weights[i] // pool), rest)
            given[i] = given[i] + addition
            rest = rest - addition
    return np.array(given)


def gaussian(key, dims, scale, reach, pieces=(), held_as=jnp.bfloat16):
    factor_of = steps_of(key, dims, pieces, -0.22, 0.18) if pieces else 1.0
    entries = jax.random.normal(key, dims, jnp.float32) * scale * factor_of
    return jnp.minimum(jnp.maximum(entries, -reach), reach).astype(held_as)


def setup_inputs(seed: int = 0) -> dict:
    streams_of = jax.random.split(jax.random.key(seed), 18)
    attn_context = gaussian(streams_of[0], (TOKENS, QH * HD), 1.0, 6.0, ((0, 8), (1, 4)))
    residual = draw_residual(jax.random.fold_in(streams_of[17], 71), 0)
    w_out = gaussian(streams_of[2], (QH * HD, D), (QH * HD) ** -0.5, 0.09375, ((0, 4),))
    gain_post = jnp.clip(1.0 + 0.1 * jax.random.normal(streams_of[3], (D,), jnp.float32), 0.5, 1.5).astype(jnp.bfloat16)
    gain_input = jnp.clip(1.0 + 0.1 * jax.random.normal(streams_of[4], (D,), jnp.float32), 0.5, 1.5).astype(jnp.bfloat16)
    routes_keys = jax.random.split(jax.random.fold_in(streams_of[5], 1), TOKENS // TOK_DEV)
    routes_turns = jax.random.permutation(jax.random.fold_in(streams_of[5], 3), TOKENS // TOK_DEV)
    routes = jax.vmap(lambda own, number: assign_block(jax.random.fold_in(streams_of[5], 2), own, number, TOK_DEV, EXPERTS, TOP, CAP, 2))(routes_keys, routes_turns).reshape((TOKENS, TOP))
    router_scores = jnp.clip(jnp.exp(math.log(1.0) - 3.912023 * jax.random.uniform(streams_of[6], (TOKENS, TOP), jnp.float32) ** steps_of(streams_of[6], (TOKENS, TOP), ((0, 8),), -0.2, 0.2)), 0.02, 1.0)
    w_gate = gaussian(streams_of[7], (2 * EXPERTS, D, HALF), D ** -0.5, 0.125, ((0, 32),))
    w_up = gaussian(streams_of[8], (2 * EXPERTS, D, HALF), D ** -0.5, 0.125, ((0, 32),))
    w_down = gaussian(streams_of[9], (2 * EXPERTS, HALF, D), FF ** -0.5, 0.21875, ((0, 32),))
    w_query = draw_w_query(jax.random.fold_in(streams_of[17], 71), 0)
    w_keyval = draw_w_keyval(jax.random.fold_in(streams_of[17], 71), 0)
    segment_ids = jax.vmap(lambda own: jnp.searchsorted(jnp.cumsum(uneven_parts(own, 4, PRE_DEV, PRE_DEV // 2, 2)), jnp.arange(PRE_DEV), side="right"))(jax.random.split(streams_of[12], N_ROW)).reshape((N_ROW, PRE_DEV)).astype(jnp.int32)
    cache_lengths = uneven_parts(streams_of[13], CACHES, CACHES * LMAX // 2, LMAX, 2).astype(jnp.int32)
    holders = jax.random.permutation(streams_of[14], CACHES).astype(jnp.int32)
    cache_keys = draw_cache_keys(jax.random.fold_in(streams_of[17], 71), 0)
    cache_values = draw_cache_values(jax.random.fold_in(streams_of[17], 71), 0)
    return dict(attn_context=attn_context, residual=residual, w_out=w_out, gain_post=gain_post, gain_input=gain_input, routes=routes, router_scores=router_scores, w_gate=w_gate, w_up=w_up, w_down=w_down, w_query=w_query, w_keyval=w_keyval, segment_ids=segment_ids, cache_lengths=cache_lengths, holders=holders, cache_keys=cache_keys, cache_values=cache_values)


EPSILON = 1e-06
ROPE_THETA = 1000000.0
NEGATIVE = -1e+30

def rms_norm(hidden, gain_vector):
    values = hidden.astype(jnp.float32)
    inverse = lax.rsqrt(lax.optimization_barrier(jnp.mean(values * values, axis=-1, keepdims=True)) + EPSILON)
    return (values * inverse * gain_vector.astype(jnp.float32)).astype(jnp.bfloat16)

def rotate(values, positions):
    head_width = values.shape[-1]
    half_width = head_width // 2
    indices = jnp.arange(half_width).astype(jnp.float32)
    inverse = ROPE_THETA ** (-2.0 * indices / head_width)
    angles = positions.astype(jnp.float32)[:, None] * inverse[None, :]
    cosine = jnp.concatenate([jnp.cos(angles), jnp.cos(angles)], axis=-1)[:, None, :]
    sine_part = jnp.concatenate([jnp.sin(angles), jnp.sin(angles)], axis=-1)[:, None, :]
    floats = values.astype(jnp.float32)
    turned = jnp.concatenate([-floats[..., half_width:], floats[..., :half_width]], axis=-1)
    return (floats * cosine + turned * sine_part).astype(jnp.bfloat16)

def segment_positions(segment_rows):
    earlier = lax.optimization_barrier(jnp.sum((segment_rows[None, :] < segment_rows[:, None]).astype(jnp.int32), axis=1))
    return jnp.arange(segment_rows.shape[0], dtype=jnp.int32) - earlier.astype(jnp.int32)

def prefill_group(items):
    queries, key_rows, value_rows, segment_rows = items
    count_rows = queries.shape[0]
    grouped = queries.astype(jnp.float32).reshape(count_rows, KVH, QH // KVH, HD)
    scores = jnp.einsum('igqd,jgd->gqij', grouped, key_rows.astype(jnp.float32)) * HD ** (-0.5)
    ordinal = jnp.arange(count_rows)
    allowed = (segment_rows[:, None] == segment_rows[None, :]) & (ordinal[None, :] <= ordinal[:, None])
    scores = jnp.where(allowed, scores, NEGATIVE)
    highest = lax.optimization_barrier(jnp.max(scores, axis=-1, keepdims=True))
    exponent = jnp.exp(scores - highest)
    probability = (exponent / lax.optimization_barrier(jnp.sum(exponent, axis=-1, keepdims=True))).astype(jnp.bfloat16)
    blended = jnp.einsum('gqij,jgd->igqd', probability.astype(jnp.float32), value_rows.astype(jnp.float32))
    return blended.reshape(count_rows, QH * HD).astype(jnp.bfloat16)

def reference(attn_context, residual, w_out, gain_post, gain_input, routes, router_scores, w_gate, w_up, w_down, w_query, w_keyval, segment_ids, cache_lengths, holders, cache_keys, cache_values):
    projected = jnp.dot(attn_context, w_out, preferred_element_type=jnp.float32)
    hidden_mid = (residual.astype(jnp.float32) + projected).astype(jnp.bfloat16)
    normed = rms_norm(hidden_mid, gain_post)
    route_weight = router_scores / lax.optimization_barrier(jnp.sum(router_scores, axis=1, keepdims=True))
    expert_ids = jnp.arange(EXPERTS, dtype=jnp.int32)
    counts = jnp.zeros((TOKENS, EXPERTS), jnp.int32)
    for choice_index in range(TOP):
        counts = counts + (routes[:, choice_index][:, None] == expert_ids[None, :]).astype(jnp.int32)
    grouped_counts = counts.reshape(N_ROW, TOK_DEV, EXPERTS)
    before = (jnp.cumsum(grouped_counts, axis=1) - grouped_counts).reshape(TOKENS, EXPERTS)
    rank = jnp.take_along_axis(before, routes, axis=1)
    group_of = (jnp.arange(TOKENS, dtype=jnp.int32) // TOK_DEV)[:, None]
    slot_index = (group_of * CAP + rank).astype(jnp.int32)
    token_ids = jnp.broadcast_to(jnp.arange(TOKENS, dtype=jnp.int32)[:, None], (TOKENS, TOP))
    table = jnp.full((EXPERTS, N_ROW * CAP), TOKENS, jnp.int32).at[routes, slot_index].set(token_ids)
    weight_table = jnp.zeros((EXPERTS, N_ROW * CAP), jnp.float32).at[routes, slot_index].set(route_weight)
    padded = jnp.concatenate([normed, jnp.zeros((1, D), jnp.bfloat16)], axis=0)

    def expert_step(total, items):
        index_rows, weight_rows, gate_pair, up_pair, down_pair = items
        chosen = padded[index_rows]
        summed = jnp.zeros((index_rows.shape[0], D), jnp.float32)
        for half_index in range(2):
            gate_part = jnp.dot(chosen, gate_pair[half_index], preferred_element_type=jnp.float32)
            up_part = jnp.dot(chosen, up_pair[half_index], preferred_element_type=jnp.float32)
            inner = (jax.nn.silu(gate_part) * up_part).astype(jnp.bfloat16)
            rounded = jnp.dot(inner, down_pair[half_index], preferred_element_type=jnp.float32).astype(jnp.bfloat16)
            summed = summed + lax.optimization_barrier(rounded).astype(jnp.float32)
        return (total.at[index_rows].add(weight_rows[:, None] * summed, mode='drop'), None)
    moe, _ = lax.scan(expert_step, jnp.zeros((TOKENS, D), jnp.float32), (table, weight_table, w_gate.reshape(EXPERTS, 2, D, HALF), w_up.reshape(EXPERTS, 2, D, HALF), w_down.reshape(EXPERTS, 2, HALF, D)))
    hidden_out = (hidden_mid.astype(jnp.float32) + moe).astype(jnp.bfloat16)
    x_in = rms_norm(hidden_out, gain_input)
    query = jnp.dot(x_in, w_query, preferred_element_type=jnp.float32).astype(jnp.bfloat16).reshape(TOKENS, QH, HD)
    keyval = jnp.dot(x_in, w_keyval, preferred_element_type=jnp.float32).astype(jnp.bfloat16).reshape(TOKENS, KVH, 2, HD)
    prompt_pos = jax.vmap(segment_positions)(segment_ids)
    position = jnp.concatenate([cache_lengths.reshape(N_ROW, DEC_DEV), prompt_pos], axis=1).reshape(TOKENS)
    query_rot = rotate(query, position)
    key_rot = rotate(keyval[:, :, 0, :], position)
    value_rows = keyval[:, :, 1, :]
    new_cache = jnp.stack([key_rot, value_rows], axis=2).reshape(TOKENS, 2 * KVH * HD)
    query_grid = query_rot.reshape(N_ROW, TOK_DEV, QH, HD)
    key_grid = key_rot.reshape(N_ROW, TOK_DEV, KVH, HD)
    value_grid = value_rows.reshape(N_ROW, TOK_DEV, KVH, HD)
    prompt_out = lax.map(prefill_group, (query_grid[:, DEC_DEV:], key_grid[:, DEC_DEV:], value_grid[:, DEC_DEV:], segment_ids))

    def decode_one(items):
        single_query, key_new, value_new, length, cache_index = items
        held_keys = cache_keys[cache_index].astype(jnp.float32).reshape(LMAX, KVH, HD)
        held_values = cache_values[cache_index].astype(jnp.float32).reshape(LMAX, KVH, HD)
        grouped = single_query.astype(jnp.float32).reshape(KVH, QH // KVH, HD)
        scores = jnp.einsum('gqd,tgd->gqt', grouped, held_keys) * HD ** (-0.5)
        valid = (jnp.arange(LMAX) < length)[None, None, :]
        scores = jnp.where(valid, scores, NEGATIVE)
        own_score = jnp.einsum('gqd,gd->gq', grouped, key_new.astype(jnp.float32)) * HD ** (-0.5)
        highest = jnp.maximum(lax.optimization_barrier(jnp.max(scores, axis=-1)), own_score)
        exponent = jnp.where(valid, jnp.exp(scores - highest[..., None]), 0.0)
        own_exp = jnp.exp(own_score - highest)
        total = lax.optimization_barrier(jnp.sum(exponent, axis=-1)) + own_exp
        blended = jnp.einsum('gqt,tgd->gqd', exponent, held_values, precision=lax.Precision.HIGHEST)
        blended = blended + own_exp[..., None] * value_new.astype(jnp.float32)[:, None, :]
        return (blended / total[..., None]).reshape(QH * HD).astype(jnp.bfloat16)
    decode_out = lax.map(decode_one, (query_grid[:, :DEC_DEV].reshape(CACHES, QH, HD), key_grid[:, :DEC_DEV].reshape(CACHES, KVH, HD), value_grid[:, :DEC_DEV].reshape(CACHES, KVH, HD), cache_lengths, holders))
    attention_out = jnp.concatenate([decode_out.reshape(N_ROW, DEC_DEV, QH * HD), prompt_out], axis=1).reshape(TOKENS, QH * HD)
    return (hidden_out, new_cache, attention_out)
```

```python
import jax
import jax.numpy as jnp
from jax import lax
from jax.sharding import PartitionSpec as P

TOP = 8
QH = 32
KVH = 4
HD = 128


EPSILON = 1e-06
ROPE_THETA = 1000000.0
NEGATIVE = -1e30
DOWN_PARTS = 2


def rms_norm(hidden, gain_vector):
    values = hidden.astype(jnp.float32)
    inverse = lax.rsqrt(jnp.mean(values * values, axis=-1, keepdims=True) + EPSILON)
    return (values * inverse * gain_vector.astype(jnp.float32)).astype(jnp.bfloat16)


def rotate(values, positions):
    head_width = values.shape[-1]
    half_width = head_width // 2
    indices = jnp.arange(half_width).astype(jnp.float32)
    inverse = ROPE_THETA ** (-2.0 * indices / head_width)
    angles = positions.astype(jnp.float32)[:, None] * inverse[None, :]
    cosine = jnp.concatenate([jnp.cos(angles), jnp.cos(angles)], axis=-1)[:, None, :]
    sine_part = jnp.concatenate([jnp.sin(angles), jnp.sin(angles)], axis=-1)[:, None, :]
    floats = values.astype(jnp.float32)
    turned = jnp.concatenate([-floats[..., half_width:], floats[..., :half_width]], axis=-1)
    return (floats * cosine + turned * sine_part).astype(jnp.bfloat16)


def segment_positions(segment_rows):
    earlier = jnp.sum((segment_rows[None, :] < segment_rows[:, None]).astype(jnp.int32), axis=1)
    return jnp.arange(segment_rows.shape[0], dtype=jnp.int32) - earlier


def line_scatter(blocks, axis):
    count = blocks.shape[0]
    index = lax.axis_index(axis)

    def own(which):
        return lax.dynamic_index_in_dim(blocks, jnp.clip(which, 0, count - 1), 0, keepdims=False)

    up = down = None
    for step in range(1, count):
        send_up, send_down = own(count - step + index), own(step - count + index)
        if up is not None:
            send_up = send_up + up.astype(jnp.float32)
            send_down = send_down + down.astype(jnp.float32)
        up = lax.ppermute(
            send_up.astype(jnp.bfloat16), axis, [(i, i + 1) for i in range(step)]
        )
        down = lax.ppermute(
            send_down.astype(jnp.bfloat16),
            axis,
            [(count - 1 - i, count - 2 - i) for i in range(step)],
        )
    return own(index) + up.astype(jnp.float32) + down.astype(jnp.float32)


def line_gather(block, axis, count):
    index = lax.axis_index(axis)
    ups, downs = [block], [block]
    for step in range(1, count):
        ups.append(lax.ppermute(ups[-1], axis, [(i, i + 1) for i in range(step - 1, count - 1)]))
        downs.append(
            lax.ppermute(
                downs[-1], axis, [(count - 1 - i, count - 2 - i) for i in range(step - 1, count - 1)]
            )
        )
    return [block] + [
        jnp.where(index >= step, ups[step], downs[count - step]) for step in range(1, count)
    ]


def gather_features(block, axis, count):
    index = lax.axis_index(axis)
    full = jnp.zeros((block.shape[0], count, block.shape[1]), block.dtype)
    for step, piece in enumerate(line_gather(block, axis, count)):
        full = lax.dynamic_update_slice_in_dim(full, piece[:, None], (index - step) % count, 1)
    return full


def row_copies(piece):
    first = [(r, r ^ (4 if r & 1 else 2)) for r in range(8)]
    second = [(r, r ^ (2 if r & 1 else 4)) for r in range(8)]
    core = [(r, r ^ 1) for r in range(8)]
    near = lax.ppermute(piece, "row", first)
    far = lax.ppermute(piece, "row", second)
    diagonal = lax.ppermute(near, "row", second)
    mine = [piece, near, far, diagonal]
    out = []
    for value in mine:
        out.extend([value, lax.ppermute(value, "row", core)])
    return out


def row_sources():
    row = lax.axis_index("row")
    one = jnp.where(row % 2 == 0, 2, 4)
    other = 6 - one
    flips = [0, 1, one, 1 + other, other, 1 + one, 6, 7]
    return [row ^ flip for flip in flips]


def experts_local(normed, routes, route_weight, w_gate, w_up, w_down, col_count, parts):
    tok_rows, model_width = normed.shape
    half = w_gate.shape[2]
    col_index = lax.axis_index("col")
    both = jnp.concatenate([w_gate[0], w_up[0]], axis=1)
    share = model_width // col_count
    down_parts = w_down[0].reshape(half, col_count, parts, share // parts)
    inners = []
    for weights, source in zip(row_copies(both), row_sources()):
        expert = (source * col_count + col_index) // 2
        factor = jnp.sum(jnp.where(routes == expert, route_weight, 0.0), axis=1, keepdims=True)
        products = jnp.dot(normed, weights, preferred_element_type=jnp.float32)
        inners.append(
            (jax.nn.silu(products[:, :half]) * products[:, half:] * factor).astype(jnp.bfloat16)
        )
    sums = []
    for part in range(parts):
        piece = down_parts[:, :, part].reshape(half, col_count * (share // parts))
        total = None
        for inner, weights in zip(inners, row_copies(piece)):
            product = jnp.dot(inner, weights, preferred_element_type=jnp.float32)
            total = product if total is None else total + product
        sums.append(total.reshape(tok_rows, col_count, share // parts))
    return sums


def experts_sent(normed, routes, route_weight, w_gate, w_up, w_down, col_count):
    col_index = lax.axis_index("col")
    row_count = lax.axis_size("row")
    tok_rows, model_width = normed.shape
    group_width = col_count // 2
    capacity = 2 * tok_rows * TOP // (row_count * group_width)
    matching = routes % group_width == col_index // 2
    target = routes // group_width
    dest_ids = jnp.arange(row_count, dtype=jnp.int32)
    hitting = matching[:, :, None] & (target[:, :, None] == dest_ids[None, None, :])
    sent_flag = jnp.sum(hitting.astype(jnp.int32), axis=1)
    sent_weight = jnp.sum(jnp.where(hitting, route_weight[:, :, None], 0.0), axis=1)
    place = jnp.cumsum(sent_flag, axis=0) - sent_flag
    dest_or_drop = jnp.where(sent_flag > 0, dest_ids[None, :], row_count)
    row_ids = jnp.broadcast_to(
        jnp.arange(tok_rows, dtype=jnp.int32)[:, None], (tok_rows, row_count)
    )
    slot_rows = (
        jnp.full((row_count, capacity), tok_rows, jnp.int32)
        .at[dest_or_drop, place]
        .set(row_ids, mode="drop")
    )
    slot_weight = (
        jnp.zeros((row_count, capacity), jnp.float32)
        .at[dest_or_drop, place]
        .set(sent_weight, mode="drop")
    )
    padded = jnp.concatenate([normed, jnp.zeros((1, model_width), jnp.bfloat16)], axis=0)
    outgoing = padded[slot_rows]
    arrived = lax.all_to_all(outgoing, "row", split_axis=0, concat_axis=0, tiled=True)
    flat_rows = arrived.reshape(-1, arrived.shape[2])
    gate_part = jnp.dot(flat_rows, w_gate[0], preferred_element_type=jnp.float32)
    up_part = jnp.dot(flat_rows, w_up[0], preferred_element_type=jnp.float32)
    inner = (jax.nn.silu(gate_part) * up_part).astype(jnp.bfloat16)
    result = jnp.dot(inner, w_down[0], preferred_element_type=jnp.float32).astype(jnp.bfloat16)
    returned = lax.all_to_all(
        result.reshape(arrived.shape), "row", split_axis=0, concat_axis=0, tiled=True
    )
    weighted = slot_weight[:, :, None] * returned.astype(jnp.float32)
    return (
        jnp.zeros((tok_rows, model_width), jnp.float32)
        .at[slot_rows.reshape(-1)]
        .add(weighted.reshape(-1, model_width), mode="drop")
    )


def shards(
    attn_context,
    residual,
    w_out,
    gain_post,
    gain_input,
    routes,
    router_scores,
    w_gate,
    w_up,
    w_down,
    w_query,
    w_keyval,
    segment_ids,
    cache_lengths,
    holders,
    cache_keys,
    cache_values,
):
    col_index = lax.axis_index("col")
    col_count = lax.axis_size("col")
    row_count = lax.axis_size("row")
    tok_rows = attn_context.shape[0]
    share_width = residual.shape[1]
    model_width = share_width * col_count
    dec_count = cache_lengths.shape[0]
    expert_count = row_count * col_count // 2
    dense = row_count == 8 and expert_count <= 2 * TOP

    holder_dev = holders // dec_count
    holder_slot = holders % dec_count
    length_box = (
        jnp.zeros((row_count, dec_count), jnp.int32).at[holder_dev, holder_slot].set(cache_lengths)
    )
    length_in = lax.all_to_all(length_box, "row", split_axis=0, concat_axis=0, tiled=True)
    slot_length = jnp.sum(length_in, axis=0)

    projected = jnp.dot(attn_context, w_out, preferred_element_type=jnp.float32)
    summed = lax.psum_scatter(
        projected.astype(jnp.bfloat16), "col", scatter_dimension=1, tiled=True
    )
    hidden_mid = (residual.astype(jnp.float32) + summed.astype(jnp.float32)).astype(jnp.bfloat16)
    full_mid = lax.all_gather(hidden_mid, "col", axis=1, tiled=True)
    normed = rms_norm(full_mid, gain_post)
    route_weight = router_scores / jnp.sum(router_scores, axis=1, keepdims=True)
    if dense:
        parts = DOWN_PARTS
        width = share_width // parts
        sums = experts_local(
            normed, routes, route_weight, w_gate, w_up, w_down, col_count, parts
        )
        outs, fulls = [], []
        for part, total in enumerate(sums):
            moe_part = line_scatter(jnp.moveaxis(total, 1, 0), "col")
            mid_part = hidden_mid[:, part * width : (part + 1) * width].astype(jnp.float32)
            out_part = (mid_part + moe_part).astype(jnp.bfloat16)
            outs.append(out_part)
            fulls.append(gather_features(out_part, "col", col_count))
        hidden_out = jnp.concatenate(outs, axis=1)
        full_out = jnp.concatenate(fulls, axis=2).reshape(tok_rows, model_width)
    else:
        partial_moe = experts_sent(
            normed, routes, route_weight, w_gate, w_up, w_down, col_count
        )
        moe_share = lax.psum_scatter(partial_moe, "col", scatter_dimension=1, tiled=True)
        hidden_out = (hidden_mid.astype(jnp.float32) + moe_share).astype(jnp.bfloat16)
        full_out = lax.all_gather(hidden_out, "col", axis=1, tiled=True)
    x_in = rms_norm(full_out, gain_input)
    heads_local = QH // col_count
    score_scale = HD ** (-0.5)
    query_local = (
        jnp.dot(x_in, w_query, preferred_element_type=jnp.float32)
        .astype(jnp.bfloat16)
        .reshape(tok_rows, heads_local, HD)
    )
    keyval_local = jnp.dot(x_in, w_keyval, preferred_element_type=jnp.float32).astype(jnp.bfloat16)
    position = jnp.concatenate([cache_lengths, segment_positions(segment_ids[0])], axis=0)
    query_rot = rotate(query_local, position)

    dec_query = query_rot[:dec_count].reshape(dec_count, heads_local * HD)
    outbox = (
        jnp.zeros((row_count, dec_count, heads_local * HD), jnp.bfloat16)
        .at[holder_dev, holder_slot]
        .set(dec_query)
    )
    outbox = jnp.broadcast_to(outbox[:, None], (row_count, col_count) + outbox.shape[1:])
    inbox = lax.all_to_all(
        outbox.reshape((row_count * col_count,) + outbox.shape[2:]),
        ("row", "col"),
        split_axis=0,
        concat_axis=0,
        tiled=True,
    ).reshape(row_count, col_count, dec_count, heads_local * HD)
    slot_query = jnp.sum(inbox.astype(jnp.float32), axis=0).astype(jnp.bfloat16)
    slot_query = jnp.moveaxis(slot_query, 0, 1).reshape(dec_count, QH * HD)

    if keyval_local.shape[1] == 2 * HD:
        my_values = keyval_local[:, HD:]
        my_keys = rotate(keyval_local[:, None, :HD], position)[:, 0]
        new_cache = jnp.concatenate([my_keys, my_values], axis=1)
    else:
        keyval_all = lax.all_gather(keyval_local, "col", axis=1, tiled=True)
        keyval_heads = keyval_all.reshape(tok_rows, KVH, 2, HD)
        key_rot = rotate(keyval_heads[:, :, 0, :], position)
        value_rows = keyval_heads[:, :, 1, :]
        cache_full = jnp.stack([key_rot, value_rows], axis=2).reshape(tok_rows, 2 * KVH * HD)
        cache_share = cache_full.shape[1] // col_count
        new_cache = lax.dynamic_slice_in_dim(cache_full, col_index * cache_share, cache_share, 1)
        head_kv = col_index * heads_local // (QH // KVH)
        my_keys = lax.dynamic_index_in_dim(key_rot, head_kv, 1, keepdims=False)
        my_values = lax.dynamic_index_in_dim(value_rows, head_kv, 1, keepdims=False)

    prompt_query = query_rot[dec_count:]
    prompt_keys = my_keys[dec_count:]
    prompt_values = my_values[dec_count:]
    prompt_rows = prompt_query.shape[0]
    scores = (
        jnp.einsum("ihd,jd->hij", prompt_query, prompt_keys, preferred_element_type=jnp.float32)
        * score_scale
    )
    ordinal = jnp.arange(prompt_rows)
    segment_rows = segment_ids[0]
    allowed = (segment_rows[:, None] == segment_rows[None, :]) & (
        ordinal[None, :] <= ordinal[:, None]
    )
    scores = jnp.where(allowed[None, :, :], scores, NEGATIVE)
    highest = jnp.max(scores, axis=-1, keepdims=True)
    exponent = jnp.exp(scores - highest)
    probability = (exponent / jnp.sum(exponent, axis=-1, keepdims=True)).astype(jnp.bfloat16)
    prompt_out = jnp.einsum(
        "hij,jd->ihd", probability, prompt_values, preferred_element_type=jnp.float32
    )
    prompt_out = prompt_out.astype(jnp.bfloat16).reshape(prompt_rows, heads_local * HD)

    span_len = cache_keys.shape[1]
    span_start = col_index * span_len
    grouped = slot_query.reshape(dec_count, KVH, QH // KVH, HD)
    held_keys = cache_keys.reshape(dec_count, span_len, KVH, HD)
    held_values = cache_values.reshape(dec_count, span_len, KVH, HD).astype(jnp.float32)
    held_scores = (
        jnp.einsum("sgqd,stgd->sgqt", grouped, held_keys, preferred_element_type=jnp.float32)
        * score_scale
    )
    valid = ((span_start + jnp.arange(span_len))[None, :] < slot_length[:, None])[:, None, None, :]
    held_scores = jnp.where(valid, held_scores, NEGATIVE)
    score_top = jnp.max(held_scores, axis=-1)
    held_exp = jnp.where(valid, jnp.exp(held_scores - score_top[..., None]), 0.0)
    weight_mass = jnp.sum(held_exp, axis=-1)
    accum_out = jnp.einsum(
        "sgqt,stgd->sgqd", held_exp, held_values, precision=lax.Precision.HIGHEST
    )

    partial_terms = jnp.concatenate(
        [accum_out, score_top[..., None], weight_mass[..., None]], axis=-1
    ).reshape(dec_count, col_count, heads_local, HD + 2)
    spread_terms = lax.all_to_all(
        jnp.moveaxis(partial_terms, 1, 0), "col", split_axis=0, concat_axis=0, tiled=True
    )
    tops = spread_terms[..., HD]
    part_top = jnp.max(tops, axis=0)
    scale_by = jnp.exp(tops - part_top[None])
    part_mass = jnp.sum(spread_terms[..., HD + 1] * scale_by, axis=0)
    part_accum = jnp.sum(spread_terms[..., :HD] * scale_by[..., None], axis=0)
    reply = jnp.concatenate([part_accum, part_top[..., None], part_mass[..., None]], axis=-1)
    back = lax.all_to_all(
        jnp.broadcast_to(reply[None], (row_count,) + reply.shape),
        "row",
        split_axis=0,
        concat_axis=0,
        tiled=True,
    )
    remote = back[holder_dev, holder_slot]
    remote_top = remote[..., HD]
    remote_mass = remote[..., HD + 1]
    remote_accum = remote[..., :HD]
    own_query = query_rot[:dec_count].astype(jnp.float32)
    own_key = my_keys[:dec_count].astype(jnp.float32)
    own_value = my_values[:dec_count].astype(jnp.float32)
    own_score = jnp.sum(own_query * own_key[:, None, :], axis=-1) * score_scale
    final_top = jnp.maximum(remote_top, own_score)
    remote_factor = jnp.exp(remote_top - final_top)
    own_factor = jnp.exp(own_score - final_top)
    numerator = (
        remote_accum * remote_factor[..., None] + own_factor[..., None] * own_value[:, None, :]
    )
    denominator = remote_mass * remote_factor + own_factor
    decode_out = (
        (numerator / denominator[..., None])
        .reshape(dec_count, heads_local * HD)
        .astype(jnp.bfloat16)
    )
    attention_out = jnp.concatenate([decode_out, prompt_out], axis=0)
    return (hidden_out, new_cache, attention_out)


def solution(mesh):
    return jax.shard_map(
        shards,
        mesh=mesh,
        in_specs=(
            P("row", "col"),
            P("row", "col"),
            P("col", None),
            P(),
            P(),
            P("row", None),
            P("row", None),
            P(("row", "col"), None, None),
            P(("row", "col"), None, None),
            P(("row", "col"), None, None),
            P(None, "col"),
            P(None, "col"),
            P("row", None),
            P("row"),
            P("row"),
            P("row", "col", None),
            P("row", "col", None),
        ),
        out_specs=(P("row", "col"), P("row", "col"), P("row", "col")),
        check_vma=False,
    )
```

```python
import jax
import jax.numpy as jnp
from jax import lax
from jax.experimental import pallas as pl
from jax.experimental.pallas import tpu as pltpu
from jax.sharding import PartitionSpec as P

TOP = 8
QH = 32
KVH = 4
HD = 128


EPSILON = 1e-06
ROPE_THETA = 1000000.0
NEGATIVE = -1e30
PARTS = (1,)
VMEM_BYTES = 52 * 1024 * 1024


def rms_norm(hidden, gain_vector):
    values = hidden.astype(jnp.float32)
    inverse = lax.rsqrt(jnp.mean(values * values, axis=-1, keepdims=True) + EPSILON)
    return (values * inverse * gain_vector.astype(jnp.float32)).astype(jnp.bfloat16)


def rotary_tables(positions):
    half_width = HD // 2
    indices = jnp.arange(half_width).astype(jnp.float32)
    inverse = ROPE_THETA ** (-2.0 * indices / HD)
    angles = positions.astype(jnp.float32)[:, None] * inverse[None, :]
    cosine, sine_part = jnp.cos(angles), jnp.sin(angles)
    return (
        jnp.concatenate([cosine, cosine], axis=-1),
        jnp.concatenate([-sine_part, sine_part], axis=-1),
    )


def rotate(values, tables):
    cosine, sine_part = (table[:, None, :] for table in tables)
    half_width = HD // 2
    floats = values.astype(jnp.float32)
    turned = jnp.concatenate([floats[..., half_width:], floats[..., :half_width]], axis=-1)
    return (floats * cosine + turned * sine_part).astype(jnp.bfloat16)


def segment_positions(segment_rows):
    earlier = jnp.sum((segment_rows[None, :] < segment_rows[:, None]).astype(jnp.int32), axis=1)
    return jnp.arange(segment_rows.shape[0], dtype=jnp.int32) - earlier


def shifted(block, axis, count, shift):
    return lax.ppermute(block, axis, [(i, (i + shift) % count) for i in range(count)])


def shared_sum(block, axis):
    count = lax.axis_size(axis)
    spread = jnp.broadcast_to(block[None], (count,) + block.shape)
    return jnp.sum(lax.all_to_all(spread, axis, 0, 0, tiled=True), axis=0)


def inner_kernel(x_ref, *refs):
    sets, outs = refs[:6], refs[6:]
    tile = outs[0].shape[1]
    weights = jnp.concatenate([sets[0][...], sets[1][...], sets[3][...], sets[4][...]], axis=1)
    products = jnp.dot(x_ref[...], weights, preferred_element_type=jnp.float32)
    for which, out in enumerate(outs):
        gate = products[:, 2 * which * tile : (2 * which + 1) * tile]
        up = products[:, (2 * which + 1) * tile : (2 * which + 2) * tile]
        out[...] = (jax.nn.silu(gate) * up * sets[3 * which + 2][...]).astype(jnp.bfloat16)


def inner_pair(normed, sets):
    tok_rows, model_width = normed.shape
    half = sets[0][0].shape[1] // 2
    tile = 128
    steps = half // tile
    gate = pl.BlockSpec((model_width, tile), lambda step: (0, step))
    up = pl.BlockSpec((model_width, tile), lambda step: (0, step + steps))
    factor = pl.BlockSpec((tok_rows, 1), lambda step: (0, 0))
    return pl.pallas_call(
        inner_kernel,
        grid=(steps,),
        out_shape=[jax.ShapeDtypeStruct((tok_rows, half), jnp.bfloat16)] * 2,
        in_specs=[pl.BlockSpec((tok_rows, model_width), lambda step: (0, 0))]
        + [gate, up, factor] * 2,
        out_specs=[pl.BlockSpec((tok_rows, tile), lambda step: (0, step))] * 2,
        compiler_params=pltpu.CompilerParams(vmem_limit_bytes=VMEM_BYTES),
        cost_estimate=pl.CostEstimate(
            flops=8 * tok_rows * model_width * half,
            bytes_accessed=2 * model_width * (tok_rows + 4 * half),
            transcendentals=2 * tok_rows * half,
        ),
    )(normed, *[value for both, factor in sets for value in (both, both, factor)])


def down_kernel(sets, *refs):
    inners, downs = refs[:sets], refs[sets : 2 * sets]
    acc = None
    for pair in range(0, sets, 2):
        left = jnp.concatenate([inners[pair][...], inners[pair + 1][...]], axis=1)
        right = jnp.concatenate([downs[pair][...], downs[pair + 1][...]], axis=0)
        product = jnp.dot(left, right, preferred_element_type=jnp.float32)
        acc = product if acc is None else acc + product
    if len(refs) == 2 * sets + 1:
        refs[-1][...] = acc
    else:
        before, total_ref, top_ref = refs[2 * sets :]
        acc = acc + before[...]
        total_ref[...] = acc.astype(jnp.bfloat16)
        top_ref[...] = acc[0 : top_ref.shape[0], :]


def down_sum(inners, downs, before=None, tops=0):
    sets = len(inners)
    tok_rows, half = inners[0].shape
    width = downs[0].shape[1]
    tile = 256

    def moving(rows):
        return pl.BlockSpec((rows, tile), lambda step: (0, step))

    whole = jax.ShapeDtypeStruct((tok_rows, width), jnp.float32)
    rounded = [
        jax.ShapeDtypeStruct((tok_rows, width), jnp.bfloat16),
        jax.ShapeDtypeStruct((tops, width), jnp.float32),
    ]
    last = before is not None
    return pl.pallas_call(
        lambda *refs: down_kernel(sets, *refs),
        grid=(width // tile,),
        out_shape=rounded if last else whole,
        in_specs=[pl.BlockSpec((tok_rows, half), lambda step: (0, 0))] * sets
        + [moving(half)] * sets
        + [moving(tok_rows)] * last,
        out_specs=[moving(tok_rows), moving(tops)] if last else moving(tok_rows),
        compiler_params=pltpu.CompilerParams(vmem_limit_bytes=VMEM_BYTES),
        cost_estimate=pl.CostEstimate(
            flops=2 * tok_rows * width * sets * half,
            bytes_accessed=2 * sets * half * (width + tok_rows) + 4 * tok_rows * width,
            transcendentals=0,
        ),
    )(*inners, *downs, *([before] if last else []))


def tail_kernel(count, parts, decs, window, col_ref, *refs):
    fulls = refs[:parts]
    (gain, wq, wkv, cosine, sine, seg_col, seg_row, dec, hidden_ref, cache_ref, out_ref) = refs[
        parts : parts + 11
    ]
    hidden, x_in, keys, values, bias = refs[parts + 11 :]
    tok_rows = x_in.shape[0]
    rows = tok_rows // count

    def turn(block):
        floats = block.astype(jnp.float32)
        turned = pltpu.roll(floats, HD // 2, 1)
        return (floats * cosine[...] + turned * sine[...]).astype(jnp.bfloat16)

    @pl.when(pl.program_id(0) == 0)
    def _():
        col = col_ref[0]
        begin = 0
        for device in range(count):
            for full in fulls:
                width = full.shape[1] // count
                hidden[:, begin : begin + width] = full[:, device * width : (device + 1) * width]
                begin += width
        for start in range(0, tok_rows, rows):
            place = slice(start, start + rows)
            floats = hidden[place, :].astype(jnp.float32)
            inverse = lax.rsqrt(jnp.mean(floats * floats, axis=-1, keepdims=True) + EPSILON)
            x_in[place, :] = (floats * inverse * gain[...].astype(jnp.float32)).astype(jnp.bfloat16)
        share = hidden_ref.shape[1]
        hidden_ref[...] = hidden[:, pl.ds(pl.multiple_of(col * share, share), share)]
        keyval = jnp.dot(x_in[...], wkv[...], preferred_element_type=jnp.float32)
        keyval = keyval.astype(jnp.bfloat16)
        keys[...] = turn(keyval[:, :HD])
        values[...] = keyval[:, HD:]
        cache_ref[:, :HD] = keys[...]
        cache_ref[:, HD:] = values[...]
        ordinal = lax.broadcasted_iota(jnp.int32, (tok_rows, tok_rows), 0)
        other = lax.broadcasted_iota(jnp.int32, (tok_rows, tok_rows), 1)
        allowed = (seg_col[...] == seg_row[...]) & (other <= ordinal)
        bias[...] = jnp.where(allowed, 0.0, NEGATIVE)

    queries = jnp.dot(x_in[...], wq[...], preferred_element_type=jnp.float32).astype(jnp.bfloat16)
    step = 128
    for head in range(wq.shape[1] // HD):
        lanes = slice(head * HD, (head + 1) * HD)
        query = turn(queries[:, lanes])
        for start in range(0, tok_rows, step):
            first = max(0, (start - window + 1) // step * step)
            stop = start + step
            scores = (
                lax.dot_general(
                    query[start:stop],
                    keys[first:stop, :],
                    (((1,), (1,)), ((), ())),
                    preferred_element_type=jnp.float32,
                )
                * HD ** (-0.5)
                + bias[start:stop, first:stop]
            )
            highest = jnp.max(scores, axis=-1, keepdims=True)
            exponent = jnp.exp(scores - highest)
            mass = jnp.sum(exponent, axis=-1, keepdims=True)
            weights = (exponent * (1.0 / mass)).astype(jnp.bfloat16)
            mixed = jnp.dot(weights, values[first:stop, :], preferred_element_type=jnp.float32)
            mixed = mixed.astype(jnp.bfloat16)
            if start == 0:
                top = lax.broadcasted_iota(jnp.int32, (16, HD), 0)
                out_ref[0:16, lanes] = jnp.where(top < decs, dec[:, lanes], mixed[0:16])
                out_ref[16:stop, lanes] = mixed[16:]
            else:
                out_ref[start:stop, lanes] = mixed


def tail(fulls, count, gain, w_query, w_keyval, cosine, sine, segments, decode_out, col_index):
    decs = decode_out.shape[0]
    tok_rows = segments.shape[0]
    model_width = w_query.shape[0]
    query_width = w_query.shape[1]
    pair = 2 * HD
    dec_rows = jnp.pad(decode_out, ((0, 16 - decs), (0, 0)))

    def fixed(shape):
        return pl.BlockSpec(shape, lambda step: (0, 0))

    def moving(shape):
        return pl.BlockSpec(shape, lambda step: (0, step))

    share = model_width // count
    return pl.pallas_call(
        lambda *refs: tail_kernel(count, len(fulls), decs, (tok_rows - decs) // 2, *refs),
        grid=(query_width // pair,),
        out_shape=[
            jax.ShapeDtypeStruct((tok_rows, share), jnp.bfloat16),
            jax.ShapeDtypeStruct((tok_rows, pair), jnp.bfloat16),
            jax.ShapeDtypeStruct((tok_rows, query_width), jnp.bfloat16),
        ],
        in_specs=[pl.BlockSpec(memory_space=pltpu.SMEM)]
        + [fixed(full.shape) for full in fulls]
        + [
            fixed((1, model_width)),
            moving((model_width, pair)),
            fixed((model_width, pair)),
            fixed((tok_rows, HD)),
            fixed((tok_rows, HD)),
            fixed((tok_rows, 1)),
            fixed((1, tok_rows)),
            moving((16, pair)),
        ],
        out_specs=[fixed((tok_rows, share)), fixed((tok_rows, pair)), moving((tok_rows, pair))],
        scratch_shapes=[
            pltpu.VMEM((tok_rows, model_width), jnp.bfloat16),
            pltpu.VMEM((tok_rows, model_width), jnp.bfloat16),
            pltpu.VMEM((tok_rows, HD), jnp.bfloat16),
            pltpu.VMEM((tok_rows, HD), jnp.bfloat16),
            pltpu.VMEM((tok_rows, tok_rows), jnp.float32),
        ],
        compiler_params=pltpu.CompilerParams(vmem_limit_bytes=VMEM_BYTES),
        cost_estimate=pl.CostEstimate(
            flops=2 * tok_rows * model_width * (query_width + pair),
            bytes_accessed=2 * model_width * (query_width + pair + 2 * tok_rows),
            transcendentals=tok_rows * tok_rows * query_width // HD,
        ),
    )(
        col_index[None],
        *fulls,
        gain[None],
        w_query,
        w_keyval,
        cosine,
        sine,
        segments[:, None],
        segments[None],
        dec_rows,
    )


def ordered(*values):
    return lax.optimization_barrier(values)


def row_pairs():
    first = [(r, r ^ (4 if r & 1 else 2)) for r in range(8)]
    second = [(r, r ^ (2 if r & 1 else 4)) for r in range(8)]
    core = [(r, r ^ 1) for r in range(8)]
    return first, second, core


def both_cores(*values):
    core = row_pairs()[2]
    out = []
    for value in values:
        out.extend([value, lax.ppermute(value, "row", core)])
    return out


def row_sources():
    row = lax.axis_index("row")
    one = jnp.where(row % 2 == 0, 2, 4)
    other = 6 - one
    flips = [0, 1, one, 1 + other, other, 1 + one, 6, 7]
    return [row ^ flip for flip in flips]


def expert_of(source, col_count):
    return (source * col_count + lax.axis_index("col")) // 2


def naming(routes, route_weight, expert):
    return jnp.sum(jnp.where(routes == expert, route_weight, 0.0), axis=1, keepdims=True)


def inner_of(rows, gate, up, factor):
    gate_part = jnp.dot(rows, gate, preferred_element_type=jnp.float32)
    up_part = jnp.dot(rows, up, preferred_element_type=jnp.float32)
    return (jax.nn.silu(gate_part) * up_part * factor).astype(jnp.bfloat16)


def experts_sent(normed, routes, route_weight, w_gate, w_up, w_down, col_count):
    col_index = lax.axis_index("col")
    row_count = lax.axis_size("row")
    tok_rows, model_width = normed.shape
    group_width = col_count // 2
    capacity = 2 * tok_rows * TOP // (row_count * group_width)
    matching = routes % group_width == col_index // 2
    target = routes // group_width
    dest_ids = jnp.arange(row_count, dtype=jnp.int32)
    hitting = matching[:, :, None] & (target[:, :, None] == dest_ids[None, None, :])
    sent_flag = jnp.sum(hitting.astype(jnp.int32), axis=1)
    sent_weight = jnp.sum(jnp.where(hitting, route_weight[:, :, None], 0.0), axis=1)
    place = jnp.cumsum(sent_flag, axis=0) - sent_flag
    dest_or_drop = jnp.where(sent_flag > 0, dest_ids[None, :], row_count)
    row_ids = jnp.broadcast_to(
        jnp.arange(tok_rows, dtype=jnp.int32)[:, None], (tok_rows, row_count)
    )
    slot_rows = (
        jnp.full((row_count, capacity), tok_rows, jnp.int32)
        .at[dest_or_drop, place]
        .set(row_ids, mode="drop")
    )
    slot_weight = (
        jnp.zeros((row_count, capacity), jnp.float32)
        .at[dest_or_drop, place]
        .set(sent_weight, mode="drop")
    )
    padded = jnp.concatenate([normed, jnp.zeros((1, model_width), jnp.bfloat16)], axis=0)
    outgoing = padded[slot_rows]
    arrived = lax.all_to_all(outgoing, "row", split_axis=0, concat_axis=0, tiled=True)
    flat_rows = arrived.reshape(-1, arrived.shape[2])
    gate_part = jnp.dot(flat_rows, w_gate[0], preferred_element_type=jnp.float32)
    up_part = jnp.dot(flat_rows, w_up[0], preferred_element_type=jnp.float32)
    inner = (jax.nn.silu(gate_part) * up_part).astype(jnp.bfloat16)
    result = jnp.dot(inner, w_down[0], preferred_element_type=jnp.float32).astype(jnp.bfloat16)
    returned = lax.all_to_all(
        result.reshape(arrived.shape), "row", split_axis=0, concat_axis=0, tiled=True
    )
    weighted = slot_weight[:, :, None] * returned.astype(jnp.float32)
    return (
        jnp.zeros((tok_rows, model_width), jnp.float32)
        .at[slot_rows.reshape(-1)]
        .add(weighted.reshape(-1, model_width), mode="drop")
    )


def prompt_attention(prompt_query, prompt_keys, prompt_values, segment_rows):
    prompt_rows = prompt_query.shape[0]
    scores = jnp.einsum(
        "ihd,jd->hij", prompt_query, prompt_keys, preferred_element_type=jnp.float32
    ) * HD ** (-0.5)
    ordinal = jnp.arange(prompt_rows)
    allowed = (segment_rows[:, None] == segment_rows[None, :]) & (
        ordinal[None, :] <= ordinal[:, None]
    )
    scores = jnp.where(allowed[None, :, :], scores, NEGATIVE)
    highest = jnp.max(scores, axis=-1, keepdims=True)
    exponent = jnp.exp(scores - highest)
    probability = (exponent / jnp.sum(exponent, axis=-1, keepdims=True)).astype(jnp.bfloat16)
    prompt_out = jnp.einsum(
        "hij,jd->ihd", probability, prompt_values, preferred_element_type=jnp.float32
    )
    return prompt_out.astype(jnp.bfloat16).reshape(prompt_rows, -1)


def shards(
    attn_context,
    residual,
    w_out,
    gain_post,
    gain_input,
    routes,
    router_scores,
    w_gate,
    w_up,
    w_down,
    w_query,
    w_keyval,
    segment_ids,
    cache_lengths,
    holders,
    cache_keys,
    cache_values,
):
    col_index = lax.axis_index("col")
    col_count = lax.axis_size("col")
    row_count = lax.axis_size("row")
    tok_rows = attn_context.shape[0]
    share_width = residual.shape[1]
    model_width = share_width * col_count
    dec_count = cache_lengths.shape[0]
    expert_count = row_count * col_count // 2
    dense = row_count == 8 and expert_count <= 2 * TOP and col_count == KVH

    holder_dev = holders // dec_count
    holder_slot = holders % dec_count
    heads_local = QH // col_count
    score_scale = HD ** (-0.5)
    prompt_pos = segment_positions(segment_ids[0])
    tables = rotary_tables(jnp.concatenate([cache_lengths, prompt_pos], axis=0))
    dec_tables = [table[:dec_count] for table in tables]

    def project(rows, weights):
        return jnp.dot(rows, weights, preferred_element_type=jnp.float32).astype(jnp.bfloat16)

    boxes = (
        (holder_dev[None, None, :] == jnp.arange(row_count)[:, None, None])
        & (holder_slot[None, None, :] == jnp.arange(dec_count)[None, :, None])
    ).astype(jnp.float32)
    length_box = jnp.sum(boxes * cache_lengths.astype(jnp.float32)[None, None, :], axis=2)
    route_weight = router_scores / jnp.sum(router_scores, axis=1, keepdims=True)
    slot_length = lax.all_to_all(length_box, "row", split_axis=0, concat_axis=0, tiled=True)
    slot_length = jnp.sum(slot_length, axis=0).astype(jnp.int32)

    projected = jnp.dot(attn_context, w_out, preferred_element_type=jnp.float32)
    summed = lax.psum_scatter(
        projected.astype(jnp.bfloat16), "col", scatter_dimension=1, tiled=True
    )
    if dense:
        first, second, _ = row_pairs()

        def to(value, pairs):
            return lax.ppermute(value, "row", pairs)

        both = jnp.concatenate([w_gate[0], w_up[0]], axis=1)
        both_near = to(both, first)
        summed, both_near = ordered(summed, both_near)
    hidden_mid = (residual.astype(jnp.float32) + summed.astype(jnp.float32)).astype(jnp.bfloat16)
    full_mid = lax.all_gather(hidden_mid, "col", axis=1, tiled=True)
    if dense:
        both_near, both_again = ordered(both_near, both)
        both_far, both_far_2 = to(both_again, second), to(both_near, second)
        normed = rms_norm(full_mid, gain_post)
        both_far, down_again = ordered(both_far, w_down[0])
        sources = row_sources()
        factors = [naming(routes, route_weight, expert_of(source, col_count)) for source in sources]
        boths = both_cores(both, both_near, both_far)
        inners = []
        for at in range(0, 6, 2):
            inners += inner_pair(normed, list(zip(boths[at : at + 2], factors[at : at + 2])))
        inners[3], both_far_2 = ordered(inners[3], both_far_2)
        inners += inner_pair(normed, list(zip(both_cores(both_far_2), factors[6:])))
        widths = [share_width * part // sum(PARTS) for part in PARTS]
        by_device = down_again.reshape(-1, col_count, share_width)
        begin = 0
        outs, fulls, dec_sums = [], [], []
        for width in widths:
            cut = by_device[:, :, begin : begin + width].reshape(-1, col_count * width)
            near, far = to(cut, first), to(cut, second)
            inners[5], near, far = ordered(inners[5], near, far)
            last = to(near, second)
            total = down_sum(inners[:6], both_cores(cut, near, far))
            total, inners[7], last = ordered(total, inners[7], last)
            last = both_cores(last)
            total, top = down_sum(inners[6:], last, total, dec_count)
            dec_sums.append(top.reshape(dec_count, col_count, width))
            moe_part = lax.psum_scatter(total, "col", scatter_dimension=1, tiled=True)
            mid_part = hidden_mid[:, begin : begin + width].astype(jnp.float32)
            outs.append((mid_part + moe_part.astype(jnp.float32)).astype(jnp.bfloat16))
            fulls.append(lax.all_gather(outs[-1], "col", axis=1, tiled=True))
            begin += width
        dec_sums = jnp.concatenate(dec_sums, axis=2).reshape(dec_count, model_width)
        dec_hidden = full_mid[:dec_count].astype(jnp.float32) + shared_sum(dec_sums, "col")
        dec_in = rms_norm(dec_hidden.astype(jnp.bfloat16), gain_input)
    else:
        normed = rms_norm(full_mid, gain_post)
        partial_moe = experts_sent(
            normed, routes, route_weight, w_gate, w_up, w_down, col_count
        )
        moe_share = lax.psum_scatter(partial_moe, "col", scatter_dimension=1, tiled=True)
        hidden_out = (hidden_mid.astype(jnp.float32) + moe_share).astype(jnp.bfloat16)
        full_out = lax.all_gather(hidden_out, "col", axis=1, tiled=True)
        x_in = rms_norm(full_out, gain_input)
        dec_in = x_in[:dec_count]
    dec_rot = rotate(project(dec_in, w_query).reshape(dec_count, heads_local, HD), dec_tables)
    dec_query = dec_rot.reshape(dec_count, heads_local * HD)
    outbox = jnp.sum(
        boxes[..., None] * dec_query.astype(jnp.float32)[None, None], axis=2
    ).astype(jnp.bfloat16)
    outbox = jnp.broadcast_to(outbox[:, None], (row_count, col_count) + outbox.shape[1:])
    inbox = lax.all_to_all(
        outbox.reshape((row_count * col_count,) + outbox.shape[2:]),
        ("row", "col"),
        split_axis=0,
        concat_axis=0,
        tiled=True,
    ).reshape(row_count, col_count, dec_count, heads_local * HD)
    slot_query = jnp.sum(inbox.astype(jnp.float32), axis=0).astype(jnp.bfloat16)
    slot_query = jnp.moveaxis(slot_query, 0, 1).reshape(dec_count, QH * HD)

    if dense:
        dec_keyval = project(dec_in, w_keyval)
        dec_keys = rotate(dec_keyval[:, None, :HD], dec_tables)[:, 0]
        dec_values = dec_keyval[:, HD:]
    else:
        query_rot = rotate(project(x_in, w_query).reshape(tok_rows, heads_local, HD), tables)
        keyval_local = project(x_in, w_keyval)
        keyval_all = lax.all_gather(keyval_local, "col", axis=1, tiled=True)
        keyval_heads = keyval_all.reshape(tok_rows, KVH, 2, HD)
        key_rot = rotate(keyval_heads[:, :, 0, :], tables)
        value_rows = keyval_heads[:, :, 1, :]
        cache_full = jnp.stack([key_rot, value_rows], axis=2).reshape(tok_rows, 2 * KVH * HD)
        cache_share = cache_full.shape[1] // col_count
        new_cache = lax.dynamic_slice_in_dim(cache_full, col_index * cache_share, cache_share, 1)
        head_kv = col_index * heads_local // (QH // KVH)
        my_keys = lax.dynamic_index_in_dim(key_rot, head_kv, 1, keepdims=False)
        my_values = lax.dynamic_index_in_dim(value_rows, head_kv, 1, keepdims=False)
        dec_keys, dec_values = my_keys[:dec_count], my_values[:dec_count]
        prompt_out = prompt_attention(
            query_rot[dec_count:], my_keys[dec_count:], my_values[dec_count:], segment_ids[0]
        )

    span_len = cache_keys.shape[1]
    span_start = col_index * span_len
    grouped = slot_query.reshape(dec_count, KVH, QH // KVH, HD)
    held_keys = cache_keys.reshape(dec_count, span_len, KVH, HD)
    held_values = cache_values.reshape(dec_count, span_len, KVH, HD).astype(jnp.float32)
    held_scores = (
        jnp.einsum("sgqd,stgd->sgqt", grouped, held_keys, preferred_element_type=jnp.float32)
        * score_scale
    )
    valid = ((span_start + jnp.arange(span_len))[None, :] < slot_length[:, None])[:, None, None, :]
    held_scores = jnp.where(valid, held_scores, NEGATIVE)
    score_top = jnp.max(held_scores, axis=-1)
    held_exp = jnp.where(valid, jnp.exp(held_scores - score_top[..., None]), 0.0)
    weight_mass = jnp.sum(held_exp, axis=-1)
    accum_out = jnp.einsum(
        "sgqt,stgd->sgqd", held_exp, held_values, precision=lax.Precision.HIGHEST
    )

    partial_terms = jnp.concatenate(
        [accum_out, score_top[..., None], weight_mass[..., None]], axis=-1
    ).reshape(dec_count, col_count, heads_local, HD + 2)
    spread_terms = lax.all_to_all(
        jnp.moveaxis(partial_terms, 1, 0), "col", split_axis=0, concat_axis=0, tiled=True
    )
    tops = spread_terms[..., HD]
    part_top = jnp.max(tops, axis=0)
    scale_by = jnp.exp(tops - part_top[None])
    part_mass = jnp.sum(spread_terms[..., HD + 1] * scale_by, axis=0)
    part_accum = jnp.sum(spread_terms[..., :HD] * scale_by[..., None], axis=0)
    reply = jnp.concatenate([part_accum, part_top[..., None], part_mass[..., None]], axis=-1)
    back = lax.all_to_all(
        jnp.broadcast_to(reply[None], (row_count,) + reply.shape),
        "row",
        split_axis=0,
        concat_axis=0,
        tiled=True,
    )
    remote = jnp.einsum("rsj,rshd->jhd", boxes, back, precision=lax.Precision.HIGHEST)
    remote_top = remote[..., HD]
    remote_mass = remote[..., HD + 1]
    remote_accum = remote[..., :HD]
    own_query = dec_rot.astype(jnp.float32)
    own_key = dec_keys.astype(jnp.float32)
    own_value = dec_values.astype(jnp.float32)
    own_score = jnp.sum(own_query * own_key[:, None, :], axis=-1) * score_scale
    final_top = jnp.maximum(remote_top, own_score)
    remote_factor = jnp.exp(remote_top - final_top)
    own_factor = jnp.exp(own_score - final_top)
    numerator = (
        remote_accum * remote_factor[..., None] + own_factor[..., None] * own_value[:, None, :]
    )
    denominator = remote_mass * remote_factor + own_factor
    decode_out = (
        (numerator / denominator[..., None])
        .reshape(dec_count, heads_local * HD)
        .astype(jnp.bfloat16)
    )
    if dense:
        segments = jnp.concatenate([jnp.full((dec_count,), -1, jnp.int32), segment_ids[0]])
        return tuple(
            tail(
                fulls,
                col_count,
                gain_input,
                w_query,
                w_keyval,
                tables[0],
                tables[1],
                segments,
                decode_out,
                col_index,
            )
        )
    attention_out = jnp.concatenate([decode_out, prompt_out], axis=0)
    return (hidden_out, new_cache, attention_out)


def solution(mesh):
    return jax.shard_map(
        shards,
        mesh=mesh,
        in_specs=(
            P("row", "col"),
            P("row", "col"),
            P("col", None),
            P(),
            P(),
            P("row", None),
            P("row", None),
            P(("row", "col"), None, None),
            P(("row", "col"), None, None),
            P(("row", "col"), None, None),
            P(None, "col"),
            P(None, "col"),
            P("row", None),
            P("row"),
            P("row"),
            P("row", "col", None),
            P("row", "col", None),
        ),
        out_specs=(P("row", "col"), P("row", "col"), P("row", "col")),
        check_vma=False,
    )
```

```python
import jax
import jax.numpy as jnp
from jax import lax
from jax.experimental import pallas as pl
from jax.experimental.pallas import tpu as pltpu
from jax.sharding import PartitionSpec as P

TOP = 8
QH = 32
KVH = 4
HD = 128


EPSILON = 1e-06
ROPE_THETA = 1000000.0
NEGATIVE = -1e30
VMEM_BYTES = 52 * 1024 * 1024


def rms_norm(hidden, gain_vector):
    values = hidden.astype(jnp.float32)
    inverse = lax.rsqrt(jnp.mean(values * values, axis=-1, keepdims=True) + EPSILON)
    return (values * inverse * gain_vector.astype(jnp.float32)).astype(jnp.bfloat16)


def rotary_tables(positions):
    half_width = HD // 2
    indices = jnp.arange(half_width).astype(jnp.float32)
    inverse = ROPE_THETA ** (-2.0 * indices / HD)
    angles = positions.astype(jnp.float32)[:, None] * inverse[None, :]
    cosine, sine_part = jnp.cos(angles), jnp.sin(angles)
    return (
        jnp.concatenate([cosine, cosine], axis=-1),
        jnp.concatenate([-sine_part, sine_part], axis=-1),
    )


def rotate(values, tables):
    cosine, sine_part = (table[:, None, :] for table in tables)
    half_width = HD // 2
    floats = values.astype(jnp.float32)
    turned = jnp.concatenate([floats[..., half_width:], floats[..., :half_width]], axis=-1)
    return (floats * cosine + turned * sine_part).astype(jnp.bfloat16)


def segment_positions(segment_rows):
    earlier = jnp.sum((segment_rows[None, :] < segment_rows[:, None]).astype(jnp.int32), axis=1)
    return jnp.arange(segment_rows.shape[0], dtype=jnp.int32) - earlier


def shifted(block, axis, count, shift):
    return lax.ppermute(block, axis, [(i, (i + shift) % count) for i in range(count)])


def shared_sum(block, axis):
    count = lax.axis_size(axis)
    spread = jnp.broadcast_to(block[None], (count,) + block.shape)
    return jnp.sum(lax.all_to_all(spread, axis, 0, 0, tiled=True).astype(jnp.float32), axis=0)


def inner_kernel(x_ref, *refs):
    sets, outs = refs[:6], refs[6:]
    tile = outs[0].shape[1]
    weights = jnp.concatenate([sets[0][...], sets[1][...], sets[3][...], sets[4][...]], axis=1)
    products = jnp.dot(x_ref[...], weights, preferred_element_type=jnp.float32)
    for which, out in enumerate(outs):
        gate = products[:, 2 * which * tile : (2 * which + 1) * tile]
        up = products[:, (2 * which + 1) * tile : (2 * which + 2) * tile]
        out[...] = (jax.nn.silu(gate) * up * sets[3 * which + 2][...]).astype(jnp.bfloat16)


def inner_pair(normed, sets):
    tok_rows, model_width = normed.shape
    tile = 128
    half = sets[0][0].shape[1]
    half = half // 2 if sets[0][0] is sets[0][1] else half
    steps = half // tile
    gate = pl.BlockSpec((model_width, tile), lambda step: (0, step))
    second = pl.BlockSpec((model_width, tile), lambda step: (0, step + steps))
    factor = pl.BlockSpec((tok_rows, 1), lambda step: (0, 0))
    specs = [
        spec for one, two, _ in sets for spec in (gate, second if one is two else gate, factor)
    ]
    return pl.pallas_call(
        inner_kernel,
        grid=(steps,),
        out_shape=[jax.ShapeDtypeStruct((tok_rows, half), jnp.bfloat16)] * 2,
        in_specs=[pl.BlockSpec((tok_rows, model_width), lambda step: (0, 0))]
        + specs,
        out_specs=[pl.BlockSpec((tok_rows, tile), lambda step: (0, step))] * 2,
        compiler_params=pltpu.CompilerParams(vmem_limit_bytes=VMEM_BYTES),
        cost_estimate=pl.CostEstimate(
            flops=tok_rows, bytes_accessed=tok_rows, transcendentals=0
        ),
    )(normed, *[value for one in sets for value in one])


def down_kernel(sets, *refs):
    inners, downs = refs[:sets], refs[sets : 2 * sets]
    acc = None
    for pair in range(0, sets, 2):
        left = jnp.concatenate([inners[pair][...], inners[pair + 1][...]], axis=1)
        right = jnp.concatenate([downs[pair][...], downs[pair + 1][...]], axis=0)
        product = jnp.dot(left, right, preferred_element_type=jnp.float32)
        acc = product if acc is None else acc + product
    if len(refs) == 2 * sets + 1:
        refs[-1][...] = acc
    else:
        total_ref, top_ref = refs[-2:]
        if len(refs) == 2 * sets + 3:
            acc = acc + refs[2 * sets][...]
        total_ref[...] = acc.astype(jnp.bfloat16)
        top_ref[...] = acc[0 : top_ref.shape[0], :]


def down_sum(inners, downs, before=None, tops=0):
    sets = len(inners)
    tok_rows, half = inners[0].shape
    width = downs[0].shape[1]
    tile = 256

    def moving(rows):
        return pl.BlockSpec((rows, tile), lambda step: (0, step))

    whole = jax.ShapeDtypeStruct((tok_rows, width), jnp.float32)
    rounded = [
        jax.ShapeDtypeStruct((tok_rows, width), jnp.bfloat16),
        jax.ShapeDtypeStruct((tops, width), jnp.float32),
    ]
    last, more = tops > 0, before is not None
    return pl.pallas_call(
        lambda *refs: down_kernel(sets, *refs),
        grid=(width // tile,),
        out_shape=rounded if last else whole,
        in_specs=[pl.BlockSpec((tok_rows, half), lambda step: (0, 0))] * sets
        + [moving(half)] * sets
        + [moving(tok_rows)] * more,
        out_specs=[moving(tok_rows), moving(tops)] if last else moving(tok_rows),
        compiler_params=pltpu.CompilerParams(vmem_limit_bytes=VMEM_BYTES),
        cost_estimate=pl.CostEstimate(
            flops=2 * tok_rows * width * sets * half,
            bytes_accessed=2 * sets * half * (width + tok_rows) + 4 * tok_rows * width,
            transcendentals=0,
        ),
    )(*inners, *downs, *([before] if more else []))


def tail_kernel(count, window, col_ref, *refs):
    (full, gain, wq, wkv, cosine, sine, seg_col, seg_row, hidden_ref, cache_ref, out_ref) = refs[:11]
    x_in, keys, values, bias = refs[11:]
    tok_rows = x_in.shape[0]
    rows = tok_rows // count

    def turn(block):
        floats = block.astype(jnp.float32)
        turned = pltpu.roll(floats, HD // 2, 1)
        return (floats * cosine[...] + turned * sine[...]).astype(jnp.bfloat16)

    @pl.when(pl.program_id(0) == 0)
    def _():
        col = col_ref[0]
        for start in range(0, tok_rows, rows):
            place = slice(start, start + rows)
            floats = full[place, :].astype(jnp.float32)
            inverse = lax.rsqrt(jnp.mean(floats * floats, axis=-1, keepdims=True) + EPSILON)
            x_in[place, :] = (floats * inverse * gain[...].astype(jnp.float32)).astype(jnp.bfloat16)
        share = hidden_ref.shape[1]
        hidden_ref[...] = full[:, pl.ds(pl.multiple_of(col * share, share), share)]
        keyval = jnp.dot(x_in[...], wkv[...], preferred_element_type=jnp.float32)
        keyval = keyval.astype(jnp.bfloat16)
        keys[...] = turn(keyval[:, :HD])
        values[...] = keyval[:, HD:]
        cache_ref[:, :HD] = keys[...]
        cache_ref[:, HD:] = values[...]
        ordinal = lax.broadcasted_iota(jnp.int32, (tok_rows, tok_rows), 0)
        other = lax.broadcasted_iota(jnp.int32, (tok_rows, tok_rows), 1)
        allowed = (seg_col[...] == seg_row[...]) & (other <= ordinal)
        bias[...] = jnp.where(allowed, 0.0, NEGATIVE)

    queries = jnp.dot(x_in[...], wq[...], preferred_element_type=jnp.float32).astype(jnp.bfloat16)
    heads = wq.shape[1] // HD
    turned = [turn(queries[:, head * HD : (head + 1) * HD]) for head in range(heads)]
    step = 128
    for start in range(0, tok_rows, step):
        first = max(0, (start - window + 1) // step * step)
        stop = start + step
        query = jnp.concatenate([head[start:stop] for head in turned], axis=0)
        scores = lax.dot_general(
            query,
            keys[first:stop, :],
            (((1,), (1,)), ((), ())),
            preferred_element_type=jnp.float32,
        ) * HD ** (-0.5)
        scores = scores.reshape(heads, step, stop - first) + bias[start:stop, first:stop][None]
        scores = scores.reshape(heads * step, stop - first)
        highest = jnp.max(scores, axis=-1, keepdims=True)
        exponent = jnp.exp(scores - highest)
        mass = jnp.sum(exponent, axis=-1, keepdims=True)
        mixed = jnp.dot(
            exponent.astype(jnp.bfloat16), values[first:stop, :], preferred_element_type=jnp.float32
        )
        mixed = (mixed * (1.0 / mass)).astype(jnp.bfloat16)
        for head in range(heads):
            out_ref[start:stop, head * HD : (head + 1) * HD] = mixed[head * step : (head + 1) * step]


def tail(full, count, gain, w_query, w_keyval, cosine, sine, segments, window, col_index):
    tok_rows = segments.shape[0]
    model_width = w_query.shape[0]
    query_width = w_query.shape[1]
    pair, some = 2 * HD, min(4 * HD, query_width)

    def fixed(shape):
        return pl.BlockSpec(shape, lambda step: (0, 0))

    def moving(shape):
        return pl.BlockSpec(shape, lambda step: (0, step))

    share = model_width // count
    return pl.pallas_call(
        lambda *refs: tail_kernel(count, window, *refs),
        grid=(query_width // some,),
        out_shape=[
            jax.ShapeDtypeStruct((tok_rows, share), jnp.bfloat16),
            jax.ShapeDtypeStruct((tok_rows, pair), jnp.bfloat16),
            jax.ShapeDtypeStruct((tok_rows, query_width), jnp.bfloat16),
        ],
        in_specs=[pl.BlockSpec(memory_space=pltpu.SMEM)]
        + [fixed(full.shape)]
        + [
            fixed((1, model_width)),
            moving((model_width, some)),
            fixed((model_width, pair)),
            fixed((tok_rows, HD)),
            fixed((tok_rows, HD)),
            fixed((tok_rows, 1)),
            fixed((1, tok_rows)),
        ],
        out_specs=[fixed((tok_rows, share)), fixed((tok_rows, pair)), moving((tok_rows, some))],
        scratch_shapes=[
            pltpu.VMEM((tok_rows, model_width), jnp.bfloat16),
            pltpu.VMEM((tok_rows, HD), jnp.bfloat16),
            pltpu.VMEM((tok_rows, HD), jnp.bfloat16),
            pltpu.VMEM((tok_rows, tok_rows), jnp.float32),
        ],
        compiler_params=pltpu.CompilerParams(vmem_limit_bytes=VMEM_BYTES),
        cost_estimate=pl.CostEstimate(
            flops=2 * tok_rows * model_width * (query_width + pair),
            bytes_accessed=2 * model_width * (query_width + pair + 2 * tok_rows),
            transcendentals=tok_rows * tok_rows * query_width // HD,
        ),
    )(
        col_index[None],
        full,
        gain[None],
        w_query,
        w_keyval,
        cosine,
        sine,
        segments[:, None],
        segments[None],
    )


def ordered(*values):
    return lax.optimization_barrier(values)


def row_pairs():
    first = [(r, r ^ (4 if r & 1 else 2)) for r in range(8)]
    second = [(r, r ^ (2 if r & 1 else 4)) for r in range(8)]
    core = [(r, r ^ 1) for r in range(8)]
    return first, second, core


def other_core(value):
    return lax.ppermute(value, "row", row_pairs()[2])


def both_cores(*values):
    return [copy for value in values for copy in (value, other_core(value))]


def row_sources():
    row = lax.axis_index("row")
    one = jnp.where(row % 2 == 0, 2, 4)
    other = 6 - one
    flips = [0, 1, one, 1 + other, other, 1 + one, 6, 7]
    return [row ^ flip for flip in flips]


def expert_of(source, col_count):
    return (source * col_count + lax.axis_index("col")) // 2


def naming(routes, route_weight, expert):
    return jnp.sum(jnp.where(routes == expert, route_weight, 0.0), axis=1, keepdims=True)


def inner_of(rows, gate, up, factor):
    gate_part = jnp.dot(rows, gate, preferred_element_type=jnp.float32)
    up_part = jnp.dot(rows, up, preferred_element_type=jnp.float32)
    return (jax.nn.silu(gate_part) * up_part * factor).astype(jnp.bfloat16)


def experts_sent(normed, routes, route_weight, w_gate, w_up, w_down, col_count):
    col_index = lax.axis_index("col")
    row_count = lax.axis_size("row")
    tok_rows, model_width = normed.shape
    group_width = col_count // 2
    capacity = 2 * tok_rows * TOP // (row_count * group_width)
    matching = routes % group_width == col_index // 2
    target = routes // group_width
    dest_ids = jnp.arange(row_count, dtype=jnp.int32)
    hitting = matching[:, :, None] & (target[:, :, None] == dest_ids[None, None, :])
    sent_flag = jnp.sum(hitting.astype(jnp.int32), axis=1)
    sent_weight = jnp.sum(jnp.where(hitting, route_weight[:, :, None], 0.0), axis=1)
    place = jnp.cumsum(sent_flag, axis=0) - sent_flag
    dest_or_drop = jnp.where(sent_flag > 0, dest_ids[None, :], row_count)
    row_ids = jnp.broadcast_to(
        jnp.arange(tok_rows, dtype=jnp.int32)[:, None], (tok_rows, row_count)
    )
    slot_rows = (
        jnp.full((row_count, capacity), tok_rows, jnp.int32)
        .at[dest_or_drop, place]
        .set(row_ids, mode="drop")
    )
    slot_weight = (
        jnp.zeros((row_count, capacity), jnp.float32)
        .at[dest_or_drop, place]
        .set(sent_weight, mode="drop")
    )
    padded = jnp.concatenate([normed, jnp.zeros((1, model_width), jnp.bfloat16)], axis=0)
    outgoing = padded[slot_rows]
    arrived = lax.all_to_all(outgoing, "row", split_axis=0, concat_axis=0, tiled=True)
    flat_rows = arrived.reshape(-1, arrived.shape[2])
    gate_part = jnp.dot(flat_rows, w_gate[0], preferred_element_type=jnp.float32)
    up_part = jnp.dot(flat_rows, w_up[0], preferred_element_type=jnp.float32)
    inner = (jax.nn.silu(gate_part) * up_part).astype(jnp.bfloat16)
    result = jnp.dot(inner, w_down[0], preferred_element_type=jnp.float32).astype(jnp.bfloat16)
    returned = lax.all_to_all(
        result.reshape(arrived.shape), "row", split_axis=0, concat_axis=0, tiled=True
    )
    weighted = slot_weight[:, :, None] * returned.astype(jnp.float32)
    return (
        jnp.zeros((tok_rows, model_width), jnp.float32)
        .at[slot_rows.reshape(-1)]
        .add(weighted.reshape(-1, model_width), mode="drop")
    )


def prompt_attention(prompt_query, prompt_keys, prompt_values, segment_rows):
    prompt_rows = prompt_query.shape[0]
    scores = jnp.einsum(
        "ihd,jd->hij", prompt_query, prompt_keys, preferred_element_type=jnp.float32
    ) * HD ** (-0.5)
    ordinal = jnp.arange(prompt_rows)
    allowed = (segment_rows[:, None] == segment_rows[None, :]) & (
        ordinal[None, :] <= ordinal[:, None]
    )
    scores = jnp.where(allowed[None, :, :], scores, NEGATIVE)
    highest = jnp.max(scores, axis=-1, keepdims=True)
    exponent = jnp.exp(scores - highest)
    probability = (exponent / jnp.sum(exponent, axis=-1, keepdims=True)).astype(jnp.bfloat16)
    prompt_out = jnp.einsum(
        "hij,jd->ihd", probability, prompt_values, preferred_element_type=jnp.float32
    )
    return prompt_out.astype(jnp.bfloat16).reshape(prompt_rows, -1)


def shards(
    attn_context,
    residual,
    w_out,
    gain_post,
    gain_input,
    routes,
    router_scores,
    w_gate,
    w_up,
    w_down,
    w_query,
    w_keyval,
    segment_ids,
    cache_lengths,
    holders,
    cache_keys,
    cache_values,
):
    col_index = lax.axis_index("col")
    col_count = lax.axis_size("col")
    row_count = lax.axis_size("row")
    tok_rows = attn_context.shape[0]
    share_width = residual.shape[1]
    model_width = share_width * col_count
    dec_count = cache_lengths.shape[0]
    expert_count = row_count * col_count // 2
    dense = row_count == 8 and expert_count <= 2 * TOP and col_count == KVH

    holder_dev = holders // dec_count
    holder_slot = holders % dec_count
    heads_local = QH // col_count
    score_scale = HD ** (-0.5)
    prompt_pos = segment_positions(segment_ids[0])
    tables = rotary_tables(jnp.concatenate([cache_lengths, prompt_pos], axis=0))
    dec_tables = [table[:dec_count] for table in tables]

    def project(rows, weights):
        return jnp.dot(rows, weights, preferred_element_type=jnp.float32).astype(jnp.bfloat16)

    boxes = (
        (holder_dev[None, None, :] == jnp.arange(row_count)[:, None, None])
        & (holder_slot[None, None, :] == jnp.arange(dec_count)[None, :, None])
    ).astype(jnp.float32)
    route_weight = router_scores / jnp.sum(router_scores, axis=1, keepdims=True)

    if dense:
        gate, up = w_gate[0], w_up[0]
    projected = jnp.dot(attn_context, w_out, preferred_element_type=jnp.float32)
    summed = lax.psum_scatter(
        projected.astype(jnp.bfloat16), "col", scatter_dimension=1, tiled=True
    )
    if dense:
        first, second, _ = row_pairs()

        def to(value, pairs):
            return lax.ppermute(value, "row", pairs)

        gate_near, up_near, gate_far = to(gate, first), to(up, first), to(gate, second)
        gate_core, up_core = other_core(gate), other_core(up)
        summed, gate_near, up_near, gate_far, gate_core, up_core = ordered(
            summed, gate_near, up_near, gate_far, gate_core, up_core
        )
    hidden_mid = (residual.astype(jnp.float32) + summed.astype(jnp.float32)).astype(jnp.bfloat16)
    full_mid = lax.all_gather(hidden_mid, "col", axis=1, tiled=True)
    if dense:
        up_near, up_again = ordered(up_near, up)
        up_far, gate_far_2, up_far_2 = to(up_again, second), to(gate_near, second), to(up_near, second)
        cores = [other_core(value) for value in (gate_near, up_near, gate_far)]
        full_mid, up_far, gate_far_2, up_far_2, down, *cores = ordered(
            full_mid, up_far, gate_far_2, up_far_2, w_down[0], *cores
        )
        normed = rms_norm(full_mid, gain_post)
        near, far = to(down, first), to(down, second)
        factors = [
            naming(routes, route_weight, expert_of(source, col_count)) for source in row_sources()
        ]

        def pair_of(gates, ups, at):
            return inner_pair(normed, list(zip(gates, ups, factors[at : at + 2])))

        inners = [
            *pair_of([gate, gate_core], [up, up_core], 0),
            *pair_of([gate_near, cores[0]], [up_near, cores[1]], 2),
            *pair_of([gate_far, cores[2]], [up_far, other_core(up_far)], 4),
        ]
        far_2_cores = [other_core(gate_far_2), other_core(up_far_2)]
        normed, inners[5], *far_2_cores = ordered(normed, inners[5], *far_2_cores)
        inners += pair_of([gate_far_2, far_2_cores[0]], [up_far_2, far_2_cores[1]], 6)
        inners[7], near, far = ordered(inners[7], near, far)
        last = to(near, second)
        partial = down_sum(inners[:6], both_cores(down, near, far))
        partial, last = ordered(partial, last)
        total, top = down_sum(inners[6:], both_cores(last), partial, dec_count)
        moe_share = lax.psum_scatter(total, "col", scatter_dimension=1, tiled=True)
        hidden_out = hidden_mid.astype(jnp.float32) + moe_share.astype(jnp.float32)
        hidden_out = hidden_out.astype(jnp.bfloat16)
        full_out = lax.all_gather(hidden_out, "col", axis=1, tiled=True)
        dec_hidden = full_mid[:dec_count].astype(jnp.float32) + shared_sum(top.astype(jnp.bfloat16), "col")
        dec_in = rms_norm(dec_hidden.astype(jnp.bfloat16), gain_input)
    else:
        normed = rms_norm(full_mid, gain_post)
        partial_moe = experts_sent(
            normed, routes, route_weight, w_gate, w_up, w_down, col_count
        )
        moe_share = lax.psum_scatter(partial_moe, "col", scatter_dimension=1, tiled=True)
        hidden_out = (hidden_mid.astype(jnp.float32) + moe_share).astype(jnp.bfloat16)
        full_out = lax.all_gather(hidden_out, "col", axis=1, tiled=True)
        x_in = rms_norm(full_out, gain_input)
        dec_in = x_in[:dec_count]
    dec_rot = rotate(project(dec_in, w_query).reshape(dec_count, heads_local, HD), dec_tables)
    lengths = jnp.stack([cache_lengths // 256, cache_lengths % 256], axis=1).astype(jnp.bfloat16)
    dec_query = jnp.concatenate(
        [
            dec_rot.reshape(dec_count, heads_local * HD),
            jnp.pad(lengths, ((0, 0), (0, HD - lengths.shape[1]))),
        ],
        axis=1,
    )
    outbox = jnp.sum(
        boxes[..., None] * dec_query.astype(jnp.float32)[None, None], axis=2
    ).astype(jnp.bfloat16)
    inbox = lax.all_to_all(outbox, "row", split_axis=0, concat_axis=0, tiled=True)
    slot_terms = jnp.sum(inbox.astype(jnp.float32), axis=0).astype(jnp.bfloat16)
    slot_terms = lax.all_to_all(
        jnp.broadcast_to(slot_terms[None], (col_count,) + slot_terms.shape),
        "col",
        split_axis=0,
        concat_axis=0,
        tiled=True,
    )
    slot_length = slot_terms[0, :, heads_local * HD :][:, :2].astype(jnp.int32)
    slot_length = slot_length[:, 0] * 256 + slot_length[:, 1]
    slot_query = slot_terms[..., : heads_local * HD]
    slot_query = jnp.moveaxis(slot_query, 0, 1).reshape(dec_count, QH * HD)

    if dense:
        dec_keyval = project(dec_in, w_keyval)
        dec_keys = rotate(dec_keyval[:, None, :HD], dec_tables)[:, 0]
        dec_values = dec_keyval[:, HD:]
    else:
        query_rot = rotate(project(x_in, w_query).reshape(tok_rows, heads_local, HD), tables)
        keyval_local = project(x_in, w_keyval)
        keyval_all = lax.all_gather(keyval_local, "col", axis=1, tiled=True)
        keyval_heads = keyval_all.reshape(tok_rows, KVH, 2, HD)
        key_rot = rotate(keyval_heads[:, :, 0, :], tables)
        value_rows = keyval_heads[:, :, 1, :]
        cache_full = jnp.stack([key_rot, value_rows], axis=2).reshape(tok_rows, 2 * KVH * HD)
        cache_share = cache_full.shape[1] // col_count
        new_cache = lax.dynamic_slice_in_dim(cache_full, col_index * cache_share, cache_share, 1)
        head_kv = col_index * heads_local // (QH // KVH)
        my_keys = lax.dynamic_index_in_dim(key_rot, head_kv, 1, keepdims=False)
        my_values = lax.dynamic_index_in_dim(value_rows, head_kv, 1, keepdims=False)
        dec_keys, dec_values = my_keys[:dec_count], my_values[:dec_count]
        prompt_out = prompt_attention(
            query_rot[dec_count:], my_keys[dec_count:], my_values[dec_count:], segment_ids[0]
        )

    span_len = cache_keys.shape[1]
    span_start = col_index * span_len
    grouped = slot_query.reshape(dec_count, KVH, QH // KVH, HD)
    held_keys = cache_keys.reshape(dec_count, span_len, KVH, HD)
    held_values = cache_values.reshape(dec_count, span_len, KVH, HD).astype(jnp.float32)
    held_scores = (
        jnp.einsum("sgqd,stgd->sgqt", grouped, held_keys, preferred_element_type=jnp.float32)
        * score_scale
    )
    valid = ((span_start + jnp.arange(span_len))[None, :] < slot_length[:, None])[:, None, None, :]
    held_scores = jnp.where(valid, held_scores, NEGATIVE)
    score_top = jnp.max(held_scores, axis=-1)
    held_exp = jnp.where(valid, jnp.exp(held_scores - score_top[..., None]), 0.0)
    weight_mass = jnp.sum(held_exp, axis=-1)
    accum_out = jnp.einsum(
        "sgqt,stgd->sgqd", held_exp, held_values, precision=lax.Precision.HIGHEST
    )

    def packed(accum, top, mass):
        notes = jnp.concatenate([top, mass], axis=-1)
        notes = jnp.pad(notes, ((0, 0),) * (notes.ndim - 1) + ((0, HD - notes.shape[-1]),))
        rows = accum.reshape(accum.shape[:-3] + (dec_count * heads_local, HD))
        return jnp.concatenate([rows, notes], axis=-2)

    def unpacked(rows):
        accum = rows[..., : dec_count * heads_local, :]
        accum = accum.reshape(rows.shape[:-2] + (dec_count, heads_local, HD))
        notes = rows[..., dec_count * heads_local :, :]
        return accum, notes[..., :heads_local], notes[..., heads_local : 2 * heads_local]

    def by_col(value):
        value = value.reshape((dec_count, col_count, heads_local) + value.shape[3:])
        return jnp.moveaxis(value, 1, 0)

    spread_terms = lax.all_to_all(
        packed(by_col(accum_out), by_col(score_top), by_col(weight_mass)),
        "col",
        split_axis=0,
        concat_axis=0,
        tiled=True,
    )
    accums, tops, masses = unpacked(spread_terms)
    part_top = jnp.max(tops, axis=0)
    scale_by = jnp.exp(tops - part_top[None])
    part_mass = jnp.sum(masses * scale_by, axis=0)
    part_accum = jnp.sum(accums * scale_by[..., None], axis=0)
    reply = packed(part_accum, part_top, part_mass)
    back = lax.all_to_all(
        jnp.broadcast_to(reply[None], (row_count,) + reply.shape),
        "row",
        split_axis=0,
        concat_axis=0,
        tiled=True,
    )
    accums, tops, masses = unpacked(back)

    def picked(value):
        mine = boxes.reshape(boxes.shape + (1,) * (value.ndim - 2))
        return jnp.sum(mine * value[:, :, None], axis=(0, 1))

    remote_top, remote_mass, remote_accum = picked(tops), picked(masses), picked(accums)
    own_query = dec_rot.astype(jnp.float32)
    own_key = dec_keys.astype(jnp.float32)
    own_value = dec_values.astype(jnp.float32)
    own_score = jnp.sum(own_query * own_key[:, None, :], axis=-1) * score_scale
    final_top = jnp.maximum(remote_top, own_score)
    remote_factor = jnp.exp(remote_top - final_top)
    own_factor = jnp.exp(own_score - final_top)
    numerator = (
        remote_accum * remote_factor[..., None] + own_factor[..., None] * own_value[:, None, :]
    )
    denominator = remote_mass * remote_factor + own_factor
    decode_out = (
        (numerator / denominator[..., None])
        .reshape(dec_count, heads_local * HD)
        .astype(jnp.bfloat16)
    )
    if dense:
        segments = jnp.concatenate([jnp.full((dec_count,), -1, jnp.int32), segment_ids[0]])
        window = segment_ids.shape[1] // 2
        hidden_out, new_cache, attention_out = tail(
            full_out,
            col_count,
            gain_input,
            w_query,
            w_keyval,
            tables[0],
            tables[1],
            segments,
            window,
            col_index,
        )
        attention_out = lax.dynamic_update_slice_in_dim(attention_out, decode_out, 0, 0)
        return (hidden_out, new_cache, attention_out)
    attention_out = jnp.concatenate([decode_out, prompt_out], axis=0)
    return (hidden_out, new_cache, attention_out)


def solution(mesh):
    return jax.shard_map(
        shards,
        mesh=mesh,
        in_specs=(
            P("row", "col"),
            P("row", "col"),
            P("col", None),
            P(),
            P(),
            P("row", None),
            P("row", None),
            P(("row", "col"), None, None),
            P(("row", "col"), None, None),
            P(("row", "col"), None, None),
            P(None, "col"),
            P(None, "col"),
            P("row", None),
            P("row"),
            P("row"),
            P("row", "col", None),
            P("row", "col", None),
        ),
        out_specs=(P("row", "col"), P("row", "col"), P("row", "col")),
        check_vma=False,
    )
```

```python
import jax
import jax.numpy as jnp
from jax import lax
from jax.experimental import pallas as pl
from jax.experimental.pallas import tpu as pltpu
from jax.sharding import PartitionSpec as P

TOP = 8
QH = 32
KVH = 4
HD = 128


EPSILON = 1e-06
ROPE_THETA = 1000000.0
NEGATIVE = -1e30
VMEM_BYTES = 60 * 1024 * 1024


def rms_norm(hidden, gain_vector):
    values = hidden.astype(jnp.float32)
    inverse = lax.rsqrt(jnp.mean(values * values, axis=-1, keepdims=True) + EPSILON)
    return (values * inverse * gain_vector.astype(jnp.float32)).astype(jnp.bfloat16)


def rotary_tables(positions):
    half_width = HD // 2
    indices = jnp.arange(half_width).astype(jnp.float32)
    inverse = ROPE_THETA ** (-2.0 * indices / HD)
    angles = positions.astype(jnp.float32)[:, None] * inverse[None, :]
    cosine, sine_part = jnp.cos(angles), jnp.sin(angles)
    return (
        jnp.concatenate([cosine, cosine], axis=-1),
        jnp.concatenate([-sine_part, sine_part], axis=-1),
    )


def rotate(values, tables):
    cosine, sine_part = (table[:, None, :] for table in tables)
    half_width = HD // 2
    floats = values.astype(jnp.float32)
    turned = jnp.concatenate([floats[..., half_width:], floats[..., :half_width]], axis=-1)
    return (floats * cosine + turned * sine_part).astype(jnp.bfloat16)


def segment_positions(segment_rows):
    earlier = jnp.sum((segment_rows[None, :] < segment_rows[:, None]).astype(jnp.int32), axis=1)
    return jnp.arange(segment_rows.shape[0], dtype=jnp.int32) - earlier


def shifted(block, axis, count, shift):
    return lax.ppermute(block, axis, [(i, (i + shift) % count) for i in range(count)])


def shared_sum(block, axis):
    count = lax.axis_size(axis)
    spread = jnp.broadcast_to(block[None], (count,) + block.shape)
    return jnp.sum(lax.all_to_all(spread, axis, 0, 0, tiled=True).astype(jnp.float32), axis=0)


def inner_kernel(sets, at, x_ref, factor_ref, *refs):
    outs = refs[2 * sets :]
    tile = outs[0].shape[1]
    for pair in range(0, sets, 2):
        weights = jnp.concatenate([ref[...] for ref in refs[2 * pair : 2 * pair + 4]], axis=1)
        products = jnp.dot(x_ref[...], weights, preferred_element_type=jnp.float32)
        for which in range(2):
            gate = products[:, 2 * which * tile : (2 * which + 1) * tile]
            up = products[:, (2 * which + 1) * tile : (2 * which + 2) * tile]
            place = at + pair + which
            inner = jax.nn.silu(gate) * up * factor_ref[:, place : place + 1]
            outs[pair + which][...] = inner.astype(jnp.bfloat16)


def inner_of(normed, factors, gates, ups, at):
    tok_rows, model_width = normed.shape
    half = gates[0].shape[1]
    tile = 128
    sets = len(gates)
    moving = pl.BlockSpec((model_width, tile), lambda step: (0, step))

    def fixed(shape):
        return pl.BlockSpec(shape, lambda step: (0, 0))

    return list(
        pl.pallas_call(
            lambda *refs: inner_kernel(sets, at, *refs),
            grid=(half // tile,),
            out_shape=[jax.ShapeDtypeStruct((tok_rows, half), jnp.bfloat16)] * sets,
            in_specs=[fixed(normed.shape), fixed(factors.shape)] + [moving] * 2 * sets,
            out_specs=[pl.BlockSpec((tok_rows, tile), lambda step: (0, step))] * sets,
            compiler_params=pltpu.CompilerParams(vmem_limit_bytes=VMEM_BYTES),
            cost_estimate=pl.CostEstimate(
                flops=tok_rows, bytes_accessed=tok_rows, transcendentals=0
            ),
        )(normed, factors, *[value for both in zip(gates, ups) for value in both])
    )


def down_kernel(sets, *refs):
    inners, downs = refs[:sets], refs[sets : 2 * sets]
    acc = None
    for pair in range(0, sets, 2):
        left = jnp.concatenate([inners[pair][...], inners[pair + 1][...]], axis=1)
        right = jnp.concatenate([downs[pair][...], downs[pair + 1][...]], axis=0)
        product = jnp.dot(left, right, preferred_element_type=jnp.float32)
        acc = product if acc is None else acc + product
    if len(refs) == 2 * sets + 1:
        refs[-1][...] = acc
    else:
        total_ref, top_ref = refs[-2:]
        if len(refs) == 2 * sets + 3:
            acc = acc + refs[2 * sets][...]
        total_ref[...] = acc.astype(jnp.bfloat16)
        top_ref[...] = acc[0 : top_ref.shape[0], :]


def down_sum(inners, downs, before=None, tops=0):
    sets = len(inners)
    tok_rows, half = inners[0].shape
    width = downs[0].shape[1]
    tile = 256

    def moving(rows):
        return pl.BlockSpec((rows, tile), lambda step: (0, step))

    whole = jax.ShapeDtypeStruct((tok_rows, width), jnp.float32)
    rounded = [
        jax.ShapeDtypeStruct((tok_rows, width), jnp.bfloat16),
        jax.ShapeDtypeStruct((tops, width), jnp.float32),
    ]
    last, more = tops > 0, before is not None
    return pl.pallas_call(
        lambda *refs: down_kernel(sets, *refs),
        grid=(width // tile,),
        out_shape=rounded if last else whole,
        in_specs=[pl.BlockSpec((tok_rows, half), lambda step: (0, 0))] * sets
        + [moving(half)] * sets
        + [moving(tok_rows)] * more,
        out_specs=[moving(tok_rows), moving(tops)] if last else moving(tok_rows),
        compiler_params=pltpu.CompilerParams(vmem_limit_bytes=VMEM_BYTES),
        cost_estimate=pl.CostEstimate(
            flops=2 * tok_rows * width * sets * half,
            bytes_accessed=2 * sets * half * (width + tok_rows) + 4 * tok_rows * width,
            transcendentals=0,
        ),
    )(*inners, *downs, *([before] if more else []))


def tail_kernel(count, window, col_ref, *refs):
    (full, gain, wq, wkv, cosine, sine, seg_col, seg_row, hidden_ref, cache_ref, out_ref) = refs[:11]
    x_in, keys, values, bias = refs[11:]
    tok_rows = x_in.shape[0]
    rows = tok_rows // count

    def turn(block):
        floats = block.astype(jnp.float32)
        turned = pltpu.roll(floats, HD // 2, 1)
        return (floats * cosine[...] + turned * sine[...]).astype(jnp.bfloat16)

    @pl.when(pl.program_id(0) == 0)
    def _():
        col = col_ref[0]
        for start in range(0, tok_rows, rows):
            place = slice(start, start + rows)
            floats = full[place, :].astype(jnp.float32)
            inverse = lax.rsqrt(jnp.mean(floats * floats, axis=-1, keepdims=True) + EPSILON)
            x_in[place, :] = (floats * inverse * gain[...].astype(jnp.float32)).astype(jnp.bfloat16)
        share = hidden_ref.shape[1]
        hidden_ref[...] = full[:, pl.ds(pl.multiple_of(col * share, share), share)]
        keyval = jnp.dot(x_in[...], wkv[...], preferred_element_type=jnp.float32)
        keyval = keyval.astype(jnp.bfloat16)
        keys[...] = turn(keyval[:, :HD])
        values[...] = keyval[:, HD:]
        cache_ref[:, :HD] = keys[...]
        cache_ref[:, HD:] = values[...]
        ordinal = lax.broadcasted_iota(jnp.int32, (tok_rows, tok_rows), 0)
        other = lax.broadcasted_iota(jnp.int32, (tok_rows, tok_rows), 1)
        allowed = (seg_col[...] == seg_row[...]) & (other <= ordinal)
        bias[...] = jnp.where(allowed, 0.0, NEGATIVE)

    queries = jnp.dot(x_in[...], wq[...], preferred_element_type=jnp.float32).astype(jnp.bfloat16)
    heads = wq.shape[1] // HD
    turned = [turn(queries[:, head * HD : (head + 1) * HD]) for head in range(heads)]
    step = 128
    for start in range(0, tok_rows, step):
        first = max(0, (start - window + 1) // step * step)
        stop = start + step
        query = jnp.concatenate([head[start:stop] for head in turned], axis=0)
        scores = lax.dot_general(
            query,
            keys[first:stop, :],
            (((1,), (1,)), ((), ())),
            preferred_element_type=jnp.float32,
        ) * HD ** (-0.5)
        scores = scores.reshape(heads, step, stop - first) + bias[start:stop, first:stop][None]
        scores = scores.reshape(heads * step, stop - first)
        highest = jnp.max(scores, axis=-1, keepdims=True)
        exponent = jnp.exp(scores - highest)
        mass = jnp.sum(exponent, axis=-1, keepdims=True)
        mixed = jnp.dot(
            exponent.astype(jnp.bfloat16), values[first:stop, :], preferred_element_type=jnp.float32
        )
        mixed = (mixed * (1.0 / mass)).astype(jnp.bfloat16)
        for head in range(heads):
            out_ref[start:stop, head * HD : (head + 1) * HD] = mixed[head * step : (head + 1) * step]


def tail(full, count, gain, w_query, w_keyval, cosine, sine, segments, window, col_index):
    tok_rows = segments.shape[0]
    model_width = w_query.shape[0]
    query_width = w_query.shape[1]
    pair, some = 2 * HD, min(4 * HD, query_width)

    def fixed(shape):
        return pl.BlockSpec(shape, lambda step: (0, 0))

    def moving(shape):
        return pl.BlockSpec(shape, lambda step: (0, step))

    share = model_width // count
    return pl.pallas_call(
        lambda *refs: tail_kernel(count, window, *refs),
        grid=(query_width // some,),
        out_shape=[
            jax.ShapeDtypeStruct((tok_rows, share), jnp.bfloat16),
            jax.ShapeDtypeStruct((tok_rows, pair), jnp.bfloat16),
            jax.ShapeDtypeStruct((tok_rows, query_width), jnp.bfloat16),
        ],
        in_specs=[pl.BlockSpec(memory_space=pltpu.SMEM)]
        + [fixed(full.shape)]
        + [
            fixed((1, model_width)),
            moving((model_width, some)),
            fixed((model_width, pair)),
            fixed((tok_rows, HD)),
            fixed((tok_rows, HD)),
            fixed((tok_rows, 1)),
            fixed((1, tok_rows)),
        ],
        out_specs=[fixed((tok_rows, share)), fixed((tok_rows, pair)), moving((tok_rows, some))],
        scratch_shapes=[
            pltpu.VMEM((tok_rows, model_width), jnp.bfloat16),
            pltpu.VMEM((tok_rows, HD), jnp.bfloat16),
            pltpu.VMEM((tok_rows, HD), jnp.bfloat16),
            pltpu.VMEM((tok_rows, tok_rows), jnp.float32),
        ],
        compiler_params=pltpu.CompilerParams(vmem_limit_bytes=VMEM_BYTES),
        cost_estimate=pl.CostEstimate(
            flops=2 * tok_rows * model_width * (query_width + pair),
            bytes_accessed=2 * model_width * (query_width + pair + 2 * tok_rows),
            transcendentals=tok_rows * tok_rows * query_width // HD,
        ),
    )(
        col_index[None],
        full,
        gain[None],
        w_query,
        w_keyval,
        cosine,
        sine,
        segments[:, None],
        segments[None],
    )


def ordered(*values):
    return lax.optimization_barrier(values)


def row_pairs():
    first = [(r, r ^ (4 if r & 1 else 2)) for r in range(8)]
    second = [(r, r ^ (2 if r & 1 else 4)) for r in range(8)]
    core = [(r, r ^ 1) for r in range(8)]
    return first, second, core


def other_core(value):
    return lax.ppermute(value, "row", row_pairs()[2])


def both_cores(*values):
    return [copy for value in values for copy in (value, other_core(value))]


def row_sources():
    row = lax.axis_index("row")
    one = jnp.where(row % 2 == 0, 2, 4)
    other = 6 - one
    flips = [0, 1, one, 1 + other, other, 1 + one, 6, 7]
    return [row ^ flip for flip in flips]


def expert_of(source, col_count):
    return (source * col_count + lax.axis_index("col")) // 2


def naming(routes, route_weight, expert):
    return jnp.sum(jnp.where(routes == expert, route_weight, 0.0), axis=1, keepdims=True)


def experts_sent(normed, routes, route_weight, w_gate, w_up, w_down, col_count):
    col_index = lax.axis_index("col")
    row_count = lax.axis_size("row")
    tok_rows, model_width = normed.shape
    group_width = col_count // 2
    capacity = 2 * tok_rows * TOP // (row_count * group_width)
    matching = routes % group_width == col_index // 2
    target = routes // group_width
    dest_ids = jnp.arange(row_count, dtype=jnp.int32)
    hitting = matching[:, :, None] & (target[:, :, None] == dest_ids[None, None, :])
    sent_flag = jnp.sum(hitting.astype(jnp.int32), axis=1)
    sent_weight = jnp.sum(jnp.where(hitting, route_weight[:, :, None], 0.0), axis=1)
    place = jnp.cumsum(sent_flag, axis=0) - sent_flag
    dest_or_drop = jnp.where(sent_flag > 0, dest_ids[None, :], row_count)
    row_ids = jnp.broadcast_to(
        jnp.arange(tok_rows, dtype=jnp.int32)[:, None], (tok_rows, row_count)
    )
    slot_rows = (
        jnp.full((row_count, capacity), tok_rows, jnp.int32)
        .at[dest_or_drop, place]
        .set(row_ids, mode="drop")
    )
    slot_weight = (
        jnp.zeros((row_count, capacity), jnp.float32)
        .at[dest_or_drop, place]
        .set(sent_weight, mode="drop")
    )
    padded = jnp.concatenate([normed, jnp.zeros((1, model_width), jnp.bfloat16)], axis=0)
    outgoing = padded[slot_rows]
    arrived = lax.all_to_all(outgoing, "row", split_axis=0, concat_axis=0, tiled=True)
    flat_rows = arrived.reshape(-1, arrived.shape[2])
    gate_part = jnp.dot(flat_rows, w_gate[0], preferred_element_type=jnp.float32)
    up_part = jnp.dot(flat_rows, w_up[0], preferred_element_type=jnp.float32)
    inner = (jax.nn.silu(gate_part) * up_part).astype(jnp.bfloat16)
    result = jnp.dot(inner, w_down[0], preferred_element_type=jnp.float32).astype(jnp.bfloat16)
    returned = lax.all_to_all(
        result.reshape(arrived.shape), "row", split_axis=0, concat_axis=0, tiled=True
    )
    weighted = slot_weight[:, :, None] * returned.astype(jnp.float32)
    return (
        jnp.zeros((tok_rows, model_width), jnp.float32)
        .at[slot_rows.reshape(-1)]
        .add(weighted.reshape(-1, model_width), mode="drop")
    )


def prompt_attention(prompt_query, prompt_keys, prompt_values, segment_rows):
    prompt_rows = prompt_query.shape[0]
    scores = jnp.einsum(
        "ihd,jd->hij", prompt_query, prompt_keys, preferred_element_type=jnp.float32
    ) * HD ** (-0.5)
    ordinal = jnp.arange(prompt_rows)
    allowed = (segment_rows[:, None] == segment_rows[None, :]) & (
        ordinal[None, :] <= ordinal[:, None]
    )
    scores = jnp.where(allowed[None, :, :], scores, NEGATIVE)
    highest = jnp.max(scores, axis=-1, keepdims=True)
    exponent = jnp.exp(scores - highest)
    probability = (exponent / jnp.sum(exponent, axis=-1, keepdims=True)).astype(jnp.bfloat16)
    prompt_out = jnp.einsum(
        "hij,jd->ihd", probability, prompt_values, preferred_element_type=jnp.float32
    )
    return prompt_out.astype(jnp.bfloat16).reshape(prompt_rows, -1)


def shards(
    attn_context,
    residual,
    w_out,
    gain_post,
    gain_input,
    routes,
    router_scores,
    w_gate,
    w_up,
    w_down,
    w_query,
    w_keyval,
    segment_ids,
    cache_lengths,
    holders,
    cache_keys,
    cache_values,
):
    col_index = lax.axis_index("col")
    col_count = lax.axis_size("col")
    row_count = lax.axis_size("row")
    tok_rows = attn_context.shape[0]
    share_width = residual.shape[1]
    model_width = share_width * col_count
    dec_count = cache_lengths.shape[0]
    expert_count = row_count * col_count // 2
    dense = row_count == 8 and expert_count <= 2 * TOP and col_count == KVH

    holder_dev = holders // dec_count
    holder_slot = holders % dec_count
    heads_local = QH // col_count
    score_scale = HD ** (-0.5)
    prompt_pos = segment_positions(segment_ids[0])
    tables = rotary_tables(jnp.concatenate([cache_lengths, prompt_pos], axis=0))
    dec_tables = [table[:dec_count] for table in tables]

    def project(rows, weights):
        return jnp.dot(rows, weights, preferred_element_type=jnp.float32).astype(jnp.bfloat16)

    boxes = (
        (holder_dev[None, None, :] == jnp.arange(row_count)[:, None, None])
        & (holder_slot[None, None, :] == jnp.arange(dec_count)[None, :, None])
    ).astype(jnp.float32)
    route_weight = router_scores / jnp.sum(router_scores, axis=1, keepdims=True)

    if dense:
        gate, up = w_gate[0], w_up[0]
    projected = jnp.dot(attn_context, w_out, preferred_element_type=jnp.float32)
    summed = lax.psum_scatter(
        projected.astype(jnp.bfloat16), "col", scatter_dimension=1, tiled=True
    )
    if dense:
        first, second, _ = row_pairs()

        def to(value, pairs):
            return lax.ppermute(value, "row", pairs)

        gate_near, up_near = to(gate, first), to(up, first)
        experts = [expert_of(source, col_count) for source in row_sources()]
        factors = [naming(routes, route_weight, expert) for expert in experts]
        factors = jnp.pad(jnp.concatenate(factors, axis=1), ((0, 0), (0, 128 - len(factors))))
        gate_core, up_core = other_core(gate), other_core(up)
        width = share_width // 2
        by_device = w_down[0].reshape(-1, col_count, share_width)
        down_a, down_b = [
            by_device[:, :, begin : begin + width].reshape(-1, col_count * width)
            for begin in (0, width)
        ]
        near = to(down_a, first)
        summed, factors, gate_near, up_near, near, gate_core, up_core, down_a, down_b = ordered(
            summed, factors, gate_near, up_near, near, gate_core, up_core, down_a, down_b
        )
    hidden_mid = (residual.astype(jnp.float32) + summed.astype(jnp.float32)).astype(jnp.bfloat16)
    full_mid = lax.all_gather(hidden_mid, "col", axis=1, tiled=True)
    if dense:
        gate_near, up_near, gate_again, up_again = ordered(gate_near, up_near, gate, up)
        gate_far, up_far = to(gate_again, second), to(up_again, second)
        near_cores = [other_core(value) for value in (gate_near, up_near)]
        gate_far, gate_near, up_near = ordered(gate_far, gate_near, up_near)
        gate_far_2, up_far_2 = to(gate_near, second), to(up_near, second)
        far_cores = [other_core(value) for value in (gate_far, up_far)]
        full_mid, *cores = ordered(full_mid, *near_cores, *far_cores)
        normed = rms_norm(full_mid, gain_post)

        def sets_of(gates, ups, at):
            return inner_of(normed, factors, gates, ups, at)

        inners = sets_of(
            [gate, gate_core, gate_near, cores[0], gate_far, cores[2]],
            [up, up_core, up_near, cores[1], up_far, cores[3]],
            0,
        )
        inners[5], gate_far_2, down_a, near = ordered(inners[5], gate_far_2, down_a, near)
        far, last = to(down_a, second), to(near, second)
        inners += sets_of(
            [gate_far_2, other_core(gate_far_2)], [up_far_2, other_core(up_far_2)], 6
        )
        inners[7], far, down_b = ordered(inners[7], far, down_b)
        downs = both_cores(down_a, near, far, last)
        near, far = to(down_b, first), to(down_b, second)
        total, top = down_sum(inners, downs, None, dec_count)
        tops = [top]
        moe_parts = [lax.psum_scatter(total, "col", scatter_dimension=1, tiled=True)]
        tops[0], near = ordered(tops[0], near)
        last = to(near, second)
        partial = down_sum(inners[:6], both_cores(down_b, near, far))
        partial, last = ordered(partial, last)
        total, top = down_sum(inners[6:], both_cores(last), partial, dec_count)
        top, moe_parts[0] = ordered(top, moe_parts[0])
        tops.append(top)
        moe_parts.append(lax.psum_scatter(total, "col", scatter_dimension=1, tiled=True))
        moe_share = jnp.concatenate(moe_parts, axis=1).astype(jnp.float32)
        hidden_out = (hidden_mid.astype(jnp.float32) + moe_share).astype(jnp.bfloat16)
        full_out = lax.all_gather(hidden_out, "col", axis=1, tiled=True)
        top = jnp.concatenate([top.reshape(dec_count, col_count, width) for top in tops], axis=2)
        top = top.reshape(dec_count, model_width)
        dec_hidden = full_mid[:dec_count].astype(jnp.float32) + shared_sum(top.astype(jnp.bfloat16), "col")
        dec_in = rms_norm(dec_hidden.astype(jnp.bfloat16), gain_input)
    else:
        normed = rms_norm(full_mid, gain_post)
        partial_moe = experts_sent(
            normed, routes, route_weight, w_gate, w_up, w_down, col_count
        )
        moe_share = lax.psum_scatter(partial_moe, "col", scatter_dimension=1, tiled=True)
        hidden_out = (hidden_mid.astype(jnp.float32) + moe_share).astype(jnp.bfloat16)
        full_out = lax.all_gather(hidden_out, "col", axis=1, tiled=True)
        x_in = rms_norm(full_out, gain_input)
        dec_in = x_in[:dec_count]
    dec_rot = rotate(project(dec_in, w_query).reshape(dec_count, heads_local, HD), dec_tables)
    lengths = jnp.stack([cache_lengths // 256, cache_lengths % 256], axis=1).astype(jnp.bfloat16)
    dec_query = jnp.concatenate(
        [
            dec_rot.reshape(dec_count, heads_local * HD),
            jnp.pad(lengths, ((0, 0), (0, HD - lengths.shape[1]))),
        ],
        axis=1,
    )
    outbox = jnp.sum(
        boxes[..., None] * dec_query.astype(jnp.float32)[None, None], axis=2
    ).astype(jnp.bfloat16)
    inbox = lax.all_to_all(outbox, "row", split_axis=0, concat_axis=0, tiled=True)
    slot_terms = jnp.sum(inbox.astype(jnp.float32), axis=0).astype(jnp.bfloat16)
    slot_terms = lax.all_to_all(
        jnp.broadcast_to(slot_terms[None], (col_count,) + slot_terms.shape),
        "col",
        split_axis=0,
        concat_axis=0,
        tiled=True,
    )
    slot_length = slot_terms[0, :, heads_local * HD :][:, :2].astype(jnp.int32)
    slot_length = slot_length[:, 0] * 256 + slot_length[:, 1]
    slot_query = slot_terms[..., : heads_local * HD]
    slot_query = jnp.moveaxis(slot_query, 0, 1).reshape(dec_count, QH * HD)

    if dense:
        dec_keyval = project(dec_in, w_keyval)
        dec_keys = rotate(dec_keyval[:, None, :HD], dec_tables)[:, 0]
        dec_values = dec_keyval[:, HD:]
    else:
        query_rot = rotate(project(x_in, w_query).reshape(tok_rows, heads_local, HD), tables)
        keyval_local = project(x_in, w_keyval)
        keyval_all = lax.all_gather(keyval_local, "col", axis=1, tiled=True)
        keyval_heads = keyval_all.reshape(tok_rows, KVH, 2, HD)
        key_rot = rotate(keyval_heads[:, :, 0, :], tables)
        value_rows = keyval_heads[:, :, 1, :]
        cache_full = jnp.stack([key_rot, value_rows], axis=2).reshape(tok_rows, 2 * KVH * HD)
        cache_share = cache_full.shape[1] // col_count
        new_cache = lax.dynamic_slice_in_dim(cache_full, col_index * cache_share, cache_share, 1)
        head_kv = col_index * heads_local // (QH // KVH)
        my_keys = lax.dynamic_index_in_dim(key_rot, head_kv, 1, keepdims=False)
        my_values = lax.dynamic_index_in_dim(value_rows, head_kv, 1, keepdims=False)
        dec_keys, dec_values = my_keys[:dec_count], my_values[:dec_count]
        prompt_out = prompt_attention(
            query_rot[dec_count:], my_keys[dec_count:], my_values[dec_count:], segment_ids[0]
        )

    span_len = cache_keys.shape[1]
    span_start = col_index * span_len
    grouped = slot_query.reshape(dec_count, KVH, QH // KVH, HD)
    held_keys = cache_keys.reshape(dec_count, span_len, KVH, HD)
    held_values = cache_values.reshape(dec_count, span_len, KVH, HD).astype(jnp.float32)
    held_scores = (
        jnp.einsum("sgqd,stgd->sgqt", grouped, held_keys, preferred_element_type=jnp.float32)
        * score_scale
    )
    valid = ((span_start + jnp.arange(span_len))[None, :] < slot_length[:, None])[:, None, None, :]
    held_scores = jnp.where(valid, held_scores, NEGATIVE)
    score_top = jnp.max(held_scores, axis=-1)
    held_exp = jnp.where(valid, jnp.exp(held_scores - score_top[..., None]), 0.0)
    weight_mass = jnp.sum(held_exp, axis=-1)
    accum_out = jnp.einsum(
        "sgqt,stgd->sgqd", held_exp, held_values, precision=lax.Precision.HIGHEST
    )

    def packed(accum, top, mass):
        notes = jnp.concatenate([top, mass], axis=-1)
        notes = jnp.pad(notes, ((0, 0),) * (notes.ndim - 1) + ((0, HD - notes.shape[-1]),))
        rows = accum.reshape(accum.shape[:-3] + (dec_count * heads_local, HD))
        return jnp.concatenate([rows, notes], axis=-2)

    def unpacked(rows):
        accum = rows[..., : dec_count * heads_local, :]
        accum = accum.reshape(rows.shape[:-2] + (dec_count, heads_local, HD))
        notes = rows[..., dec_count * heads_local :, :]
        return accum, notes[..., :heads_local], notes[..., heads_local : 2 * heads_local]

    def by_col(value):
        value = value.reshape((dec_count, col_count, heads_local) + value.shape[3:])
        return jnp.moveaxis(value, 1, 0)

    spread_terms = lax.all_to_all(
        packed(by_col(accum_out), by_col(score_top), by_col(weight_mass)),
        "col",
        split_axis=0,
        concat_axis=0,
        tiled=True,
    )
    accums, tops, masses = unpacked(spread_terms)
    part_top = jnp.max(tops, axis=0)
    scale_by = jnp.exp(tops - part_top[None])
    part_mass = jnp.sum(masses * scale_by, axis=0)
    part_accum = jnp.sum(accums * scale_by[..., None], axis=0)
    reply = packed(part_accum, part_top, part_mass)
    back = lax.all_to_all(
        jnp.broadcast_to(reply[None], (row_count,) + reply.shape),
        "row",
        split_axis=0,
        concat_axis=0,
        tiled=True,
    )
    accums, tops, masses = unpacked(back)

    def picked(value):
        mine = boxes.reshape(boxes.shape + (1,) * (value.ndim - 2))
        return jnp.sum(mine * value[:, :, None], axis=(0, 1))

    remote_top, remote_mass, remote_accum = picked(tops), picked(masses), picked(accums)
    own_query = dec_rot.astype(jnp.float32)
    own_key = dec_keys.astype(jnp.float32)
    own_value = dec_values.astype(jnp.float32)
    own_score = jnp.sum(own_query * own_key[:, None, :], axis=-1) * score_scale
    final_top = jnp.maximum(remote_top, own_score)
    remote_factor = jnp.exp(remote_top - final_top)
    own_factor = jnp.exp(own_score - final_top)
    numerator = (
        remote_accum * remote_factor[..., None] + own_factor[..., None] * own_value[:, None, :]
    )
    denominator = remote_mass * remote_factor + own_factor
    decode_out = (
        (numerator / denominator[..., None])
        .reshape(dec_count, heads_local * HD)
        .astype(jnp.bfloat16)
    )
    if dense:
        segments = jnp.concatenate([jnp.full((dec_count,), -1, jnp.int32), segment_ids[0]])
        window = segment_ids.shape[1] // 2
        hidden_out, new_cache, attention_out = tail(
            full_out,
            col_count,
            gain_input,
            w_query,
            w_keyval,
            tables[0],
            tables[1],
            segments,
            window,
            col_index,
        )
        attention_out = lax.dynamic_update_slice_in_dim(attention_out, decode_out, 0, 0)
        return (hidden_out, new_cache, attention_out)
    attention_out = jnp.concatenate([decode_out, prompt_out], axis=0)
    return (hidden_out, new_cache, attention_out)


def solution(mesh):
    return jax.shard_map(
        shards,
        mesh=mesh,
        in_specs=(
            P("row", "col"),
            P("row", "col"),
            P("col", None),
            P(),
            P(),
            P("row", None),
            P("row", None),
            P(("row", "col"), None, None),
            P(("row", "col"), None, None),
            P(("row", "col"), None, None),
            P(None, "col"),
            P(None, "col"),
            P("row", None),
            P("row"),
            P("row"),
            P("row", "col", None),
            P("row", "col", None),
        ),
        out_specs=(P("row", "col"), P("row", "col"), P("row", "col")),
        check_vma=False,
    )
```

```python
import jax
import jax.numpy as jnp
from jax import lax
from jax.experimental import pallas as pl
from jax.experimental.pallas import tpu as pltpu
from jax.sharding import PartitionSpec as P

TOP = 8
QH = 32
KVH = 4
HD = 128


EPSILON = 1e-06
ROPE_THETA = 1000000.0
NEGATIVE = -1e30
VMEM_BYTES = 60 * 1024 * 1024


def rms_norm(hidden, gain_vector):
    values = hidden.astype(jnp.float32)
    inverse = lax.rsqrt(jnp.mean(values * values, axis=-1, keepdims=True) + EPSILON)
    return (values * inverse * gain_vector.astype(jnp.float32)).astype(jnp.bfloat16)


def rotary_tables(positions):
    half_width = HD // 2
    indices = jnp.arange(half_width).astype(jnp.float32)
    inverse = ROPE_THETA ** (-2.0 * indices / HD)
    angles = positions.astype(jnp.float32)[:, None] * inverse[None, :]
    cosine, sine_part = jnp.cos(angles), jnp.sin(angles)
    return (
        jnp.concatenate([cosine, cosine], axis=-1),
        jnp.concatenate([-sine_part, sine_part], axis=-1),
    )


def rotate(values, tables):
    cosine, sine_part = (table[:, None, :] for table in tables)
    half_width = HD // 2
    floats = values.astype(jnp.float32)
    turned = jnp.concatenate([floats[..., half_width:], floats[..., :half_width]], axis=-1)
    return (floats * cosine + turned * sine_part).astype(jnp.bfloat16)


def segment_positions(segment_rows):
    earlier = jnp.sum((segment_rows[None, :] < segment_rows[:, None]).astype(jnp.int32), axis=1)
    return jnp.arange(segment_rows.shape[0], dtype=jnp.int32) - earlier


def shifted(block, axis, count, shift):
    return lax.ppermute(block, axis, [(i, (i + shift) % count) for i in range(count)])


def shifted(value, axis, shift):
    count = lax.axis_size(axis)
    return lax.ppermute(value, axis, [(i, (i + shift) % count) for i in range(count)])


def spread(blocks, axis):
    count = lax.axis_size(axis)
    index = lax.axis_index(axis)
    mine = [
        lax.dynamic_index_in_dim(blocks, (index + shift) % count, 0, keepdims=False)
        for shift in range(count)
    ]
    return jnp.stack([mine[0]] + [shifted(mine[k], axis, k) for k in range(1, count)])


def gathered(block, axis):
    count = lax.axis_size(axis)
    index = lax.axis_index(axis)
    arrived = [block] + [shifted(block, axis, k) for k in range(1, count)]
    order = jnp.stack(arrived + arrived)
    return jnp.stack(
        [
            lax.dynamic_index_in_dim(order, index - i + count, 0, keepdims=False)
            for i in range(count)
        ]
    )


def shared_sum(block, axis):
    count = lax.axis_size(axis)
    total = block.astype(jnp.float32)
    for k in range(1, count):
        total = total + shifted(block, axis, k).astype(jnp.float32)
    return total


def inner_kernel(sets, at, x_ref, factor_ref, *refs):
    outs = refs[2 * sets :]
    tile = outs[0].shape[1]
    for pair in range(0, sets, 2):
        weights = jnp.concatenate([ref[...] for ref in refs[2 * pair : 2 * pair + 4]], axis=1)
        products = jnp.dot(x_ref[...], weights, preferred_element_type=jnp.float32)
        for which in range(2):
            gate = products[:, 2 * which * tile : (2 * which + 1) * tile]
            up = products[:, (2 * which + 1) * tile : (2 * which + 2) * tile]
            place = at + pair + which
            inner = jax.nn.silu(gate) * up * factor_ref[:, place : place + 1]
            outs[pair + which][...] = inner.astype(jnp.bfloat16)


def inner_of(normed, factors, gates, ups, at):
    tok_rows, model_width = normed.shape
    half = gates[0].shape[1]
    tile = 128
    sets = len(gates)
    moving = pl.BlockSpec((model_width, tile), lambda step: (0, step))

    def fixed(shape):
        return pl.BlockSpec(shape, lambda step: (0, 0))

    return list(
        pl.pallas_call(
            lambda *refs: inner_kernel(sets, at, *refs),
            grid=(half // tile,),
            out_shape=[jax.ShapeDtypeStruct((tok_rows, half), jnp.bfloat16)] * sets,
            in_specs=[fixed(normed.shape), fixed(factors.shape)] + [moving] * 2 * sets,
            out_specs=[pl.BlockSpec((tok_rows, tile), lambda step: (0, step))] * sets,
            compiler_params=pltpu.CompilerParams(vmem_limit_bytes=VMEM_BYTES),
            cost_estimate=pl.CostEstimate(
                flops=tok_rows, bytes_accessed=tok_rows, transcendentals=0
            ),
        )(normed, factors, *[value for both in zip(gates, ups) for value in both])
    )


def down_kernel(sets, *refs):
    inners, downs = refs[:sets], refs[sets : 2 * sets]
    acc = None
    for pair in range(0, sets, 2):
        left = jnp.concatenate([inners[pair][...], inners[pair + 1][...]], axis=1)
        right = jnp.concatenate([downs[pair][...], downs[pair + 1][...]], axis=0)
        product = jnp.dot(left, right, preferred_element_type=jnp.float32)
        acc = product if acc is None else acc + product
    if len(refs) == 2 * sets + 1:
        refs[-1][...] = acc
    else:
        total_ref, top_ref = refs[-2:]
        if len(refs) == 2 * sets + 3:
            acc = acc + refs[2 * sets][...]
        total_ref[...] = acc.astype(jnp.bfloat16)
        top_ref[...] = acc[0 : top_ref.shape[0], :]


def down_sum(inners, downs, before=None, tops=0):
    sets = len(inners)
    tok_rows, half = inners[0].shape
    width = downs[0].shape[1]
    tile = 256

    def moving(rows):
        return pl.BlockSpec((rows, tile), lambda step: (0, step))

    whole = jax.ShapeDtypeStruct((tok_rows, width), jnp.float32)
    rounded = [
        jax.ShapeDtypeStruct((tok_rows, width), jnp.bfloat16),
        jax.ShapeDtypeStruct((tops, width), jnp.float32),
    ]
    last, more = tops > 0, before is not None
    return pl.pallas_call(
        lambda *refs: down_kernel(sets, *refs),
        grid=(width // tile,),
        out_shape=rounded if last else whole,
        in_specs=[pl.BlockSpec((tok_rows, half), lambda step: (0, 0))] * sets
        + [moving(half)] * sets
        + [moving(tok_rows)] * more,
        out_specs=[moving(tok_rows), moving(tops)] if last else moving(tok_rows),
        compiler_params=pltpu.CompilerParams(vmem_limit_bytes=VMEM_BYTES),
        cost_estimate=pl.CostEstimate(
            flops=2 * tok_rows * width * sets * half,
            bytes_accessed=2 * sets * half * (width + tok_rows) + 4 * tok_rows * width,
            transcendentals=0,
        ),
    )(*inners, *downs, *([before] if more else []))


def tail_kernel(window, *refs):
    (full, gain, wq, wkv, cosine, sine, seg_col, seg_row, cache_ref, out_ref) = refs[:10]
    x_in, keys, values, bias = refs[10:]
    tok_rows = x_in.shape[0]
    rows = 128

    def turn(block):
        floats = block.astype(jnp.float32)
        turned = pltpu.roll(floats, HD // 2, 1)
        return (floats * cosine[...] + turned * sine[...]).astype(jnp.bfloat16)

    @pl.when(pl.program_id(0) == 0)
    def _():
        for start in range(0, tok_rows, rows):
            place = slice(start, start + rows)
            floats = full[place, :].astype(jnp.float32)
            inverse = lax.rsqrt(jnp.mean(floats * floats, axis=-1, keepdims=True) + EPSILON)
            x_in[place, :] = (floats * inverse * gain[...].astype(jnp.float32)).astype(jnp.bfloat16)
        keyval = jnp.dot(x_in[...], wkv[...], preferred_element_type=jnp.float32)
        keyval = keyval.astype(jnp.bfloat16)
        keys[...] = turn(keyval[:, :HD])
        values[...] = keyval[:, HD:]
        cache_ref[:, :HD] = keys[...]
        cache_ref[:, HD:] = values[...]
        ordinal = lax.broadcasted_iota(jnp.int32, (tok_rows, tok_rows), 0)
        other = lax.broadcasted_iota(jnp.int32, (tok_rows, tok_rows), 1)
        allowed = (seg_col[...] == seg_row[...]) & (other <= ordinal)
        bias[...] = jnp.where(allowed, 0.0, NEGATIVE)

    queries = jnp.dot(x_in[...], wq[...], preferred_element_type=jnp.float32).astype(jnp.bfloat16)
    heads = wq.shape[1] // HD
    turned = [turn(queries[:, head * HD : (head + 1) * HD]) for head in range(heads)]
    step = 128
    for start in range(0, tok_rows, step):
        first = max(0, (start - window + 1) // step * step)
        stop = start + step
        query = jnp.concatenate([head[start:stop] for head in turned], axis=0)
        scores = lax.dot_general(
            query,
            keys[first:stop, :],
            (((1,), (1,)), ((), ())),
            preferred_element_type=jnp.float32,
        ) * HD ** (-0.5)
        scores = scores.reshape(heads, step, stop - first) + bias[start:stop, first:stop][None]
        scores = scores.reshape(heads * step, stop - first)
        highest = jnp.max(scores, axis=-1, keepdims=True)
        exponent = jnp.exp(scores - highest)
        mass = jnp.sum(exponent, axis=-1, keepdims=True)
        mixed = jnp.dot(
            exponent.astype(jnp.bfloat16), values[first:stop, :], preferred_element_type=jnp.float32
        )
        mixed = (mixed * (1.0 / mass)).astype(jnp.bfloat16)
        for head in range(heads):
            out_ref[start:stop, head * HD : (head + 1) * HD] = mixed[head * step : (head + 1) * step]


def tail(full, gain, w_query, w_keyval, cosine, sine, segments, window):
    tok_rows = segments.shape[0]
    model_width = w_query.shape[0]
    query_width = w_query.shape[1]
    pair, some = 2 * HD, min(4 * HD, query_width)

    def fixed(shape):
        return pl.BlockSpec(shape, lambda step: (0, 0))

    def moving(shape):
        return pl.BlockSpec(shape, lambda step: (0, step))

    return pl.pallas_call(
        lambda *refs: tail_kernel(window, *refs),
        grid=(query_width // some,),
        out_shape=[
            jax.ShapeDtypeStruct((tok_rows, pair), jnp.bfloat16),
            jax.ShapeDtypeStruct((tok_rows, query_width), jnp.bfloat16),
        ],
        in_specs=[
            fixed(full.shape),
            fixed((1, model_width)),
            moving((model_width, some)),
            fixed((model_width, pair)),
            fixed((tok_rows, HD)),
            fixed((tok_rows, HD)),
            fixed((tok_rows, 1)),
            fixed((1, tok_rows)),
        ],
        out_specs=[fixed((tok_rows, pair)), moving((tok_rows, some))],
        scratch_shapes=[
            pltpu.VMEM((tok_rows, model_width), jnp.bfloat16),
            pltpu.VMEM((tok_rows, HD), jnp.bfloat16),
            pltpu.VMEM((tok_rows, HD), jnp.bfloat16),
            pltpu.VMEM((tok_rows, tok_rows), jnp.float32),
        ],
        compiler_params=pltpu.CompilerParams(vmem_limit_bytes=VMEM_BYTES),
        cost_estimate=pl.CostEstimate(
            flops=2 * tok_rows * model_width * (query_width + pair),
            bytes_accessed=2 * model_width * (query_width + pair + 2 * tok_rows),
            transcendentals=tok_rows * tok_rows * query_width // HD,
        ),
    )(
        full,
        gain[None],
        w_query,
        w_keyval,
        cosine,
        sine,
        segments[:, None],
        segments[None],
    )


def ordered(*values):
    return lax.optimization_barrier(values)


def row_pairs():
    first = [(r, r ^ (4 if r & 1 else 2)) for r in range(8)]
    second = [(r, r ^ (2 if r & 1 else 4)) for r in range(8)]
    core = [(r, r ^ 1) for r in range(8)]
    return first, second, core


def other_core(value):
    return lax.ppermute(value, "row", row_pairs()[2])


def both_cores(*values):
    return [copy for value in values for copy in (value, other_core(value))]


def row_sources():
    row = lax.axis_index("row")
    one = jnp.where(row % 2 == 0, 2, 4)
    other = 6 - one
    flips = [0, 1, one, 1 + other, other, 1 + one, 6, 7]
    return [row ^ flip for flip in flips]


def expert_of(source, col_count):
    return (source * col_count + lax.axis_index("col")) // 2


def naming(routes, route_weight, expert):
    return jnp.sum(jnp.where(routes == expert, route_weight, 0.0), axis=1, keepdims=True)


def experts_sent(normed, routes, route_weight, w_gate, w_up, w_down, col_count):
    col_index = lax.axis_index("col")
    row_count = lax.axis_size("row")
    tok_rows, model_width = normed.shape
    group_width = col_count // 2
    capacity = 2 * tok_rows * TOP // (row_count * group_width)
    matching = routes % group_width == col_index // 2
    target = routes // group_width
    dest_ids = jnp.arange(row_count, dtype=jnp.int32)
    hitting = matching[:, :, None] & (target[:, :, None] == dest_ids[None, None, :])
    sent_flag = jnp.sum(hitting.astype(jnp.int32), axis=1)
    sent_weight = jnp.sum(jnp.where(hitting, route_weight[:, :, None], 0.0), axis=1)
    place = jnp.cumsum(sent_flag, axis=0) - sent_flag
    dest_or_drop = jnp.where(sent_flag > 0, dest_ids[None, :], row_count)
    row_ids = jnp.broadcast_to(
        jnp.arange(tok_rows, dtype=jnp.int32)[:, None], (tok_rows, row_count)
    )
    slot_rows = (
        jnp.full((row_count, capacity), tok_rows, jnp.int32)
        .at[dest_or_drop, place]
        .set(row_ids, mode="drop")
    )
    slot_weight = (
        jnp.zeros((row_count, capacity), jnp.float32)
        .at[dest_or_drop, place]
        .set(sent_weight, mode="drop")
    )
    padded = jnp.concatenate([normed, jnp.zeros((1, model_width), jnp.bfloat16)], axis=0)
    outgoing = padded[slot_rows]
    arrived = lax.all_to_all(outgoing, "row", split_axis=0, concat_axis=0, tiled=True)
    flat_rows = arrived.reshape(-1, arrived.shape[2])
    gate_part = jnp.dot(flat_rows, w_gate[0], preferred_element_type=jnp.float32)
    up_part = jnp.dot(flat_rows, w_up[0], preferred_element_type=jnp.float32)
    inner = (jax.nn.silu(gate_part) * up_part).astype(jnp.bfloat16)
    result = jnp.dot(inner, w_down[0], preferred_element_type=jnp.float32).astype(jnp.bfloat16)
    returned = lax.all_to_all(
        result.reshape(arrived.shape), "row", split_axis=0, concat_axis=0, tiled=True
    )
    weighted = slot_weight[:, :, None] * returned.astype(jnp.float32)
    return (
        jnp.zeros((tok_rows, model_width), jnp.float32)
        .at[slot_rows.reshape(-1)]
        .add(weighted.reshape(-1, model_width), mode="drop")
    )


def prompt_attention(prompt_query, prompt_keys, prompt_values, segment_rows):
    prompt_rows = prompt_query.shape[0]
    scores = jnp.einsum(
        "ihd,jd->hij", prompt_query, prompt_keys, preferred_element_type=jnp.float32
    ) * HD ** (-0.5)
    ordinal = jnp.arange(prompt_rows)
    allowed = (segment_rows[:, None] == segment_rows[None, :]) & (
        ordinal[None, :] <= ordinal[:, None]
    )
    scores = jnp.where(allowed[None, :, :], scores, NEGATIVE)
    highest = jnp.max(scores, axis=-1, keepdims=True)
    exponent = jnp.exp(scores - highest)
    probability = (exponent / jnp.sum(exponent, axis=-1, keepdims=True)).astype(jnp.bfloat16)
    prompt_out = jnp.einsum(
        "hij,jd->ihd", probability, prompt_values, preferred_element_type=jnp.float32
    )
    return prompt_out.astype(jnp.bfloat16).reshape(prompt_rows, -1)


def shards(
    attn_context,
    residual,
    w_out,
    gain_post,
    gain_input,
    routes,
    router_scores,
    w_gate,
    w_up,
    w_down,
    w_query,
    w_keyval,
    segment_ids,
    cache_lengths,
    holders,
    cache_keys,
    cache_values,
):
    col_index = lax.axis_index("col")
    col_count = lax.axis_size("col")
    row_count = lax.axis_size("row")
    tok_rows = attn_context.shape[0]
    share_width = residual.shape[1]
    model_width = share_width * col_count
    dec_count = cache_lengths.shape[0]
    expert_count = row_count * col_count // 2
    dense = row_count == 8 and expert_count <= 2 * TOP and col_count == KVH

    holder_dev = holders // dec_count
    holder_slot = holders % dec_count
    heads_local = QH // col_count
    score_scale = HD ** (-0.5)
    prompt_pos = segment_positions(segment_ids[0])
    tables = rotary_tables(jnp.concatenate([cache_lengths, prompt_pos], axis=0))
    dec_tables = [table[:dec_count] for table in tables]

    def project(rows, weights):
        return jnp.dot(rows, weights, preferred_element_type=jnp.float32).astype(jnp.bfloat16)

    boxes = (
        (holder_dev[None, None, :] == jnp.arange(row_count)[:, None, None])
        & (holder_slot[None, None, :] == jnp.arange(dec_count)[None, :, None])
    ).astype(jnp.float32)
    route_weight = router_scores / jnp.sum(router_scores, axis=1, keepdims=True)

    if dense:
        gate, up = w_gate[0], w_up[0]
    projected = jnp.dot(attn_context, w_out, preferred_element_type=jnp.float32)
    summed = lax.psum_scatter(
        projected.astype(jnp.bfloat16), "col", scatter_dimension=1, tiled=True
    )
    if dense:
        first, second, _ = row_pairs()

        def to(value, pairs):
            return lax.ppermute(value, "row", pairs)

        gate_near, up_near = to(gate, first), to(up, first)
        experts = [expert_of(source, col_count) for source in row_sources()]
        factors = [naming(routes, route_weight, expert) for expert in experts]
        factors = jnp.pad(jnp.concatenate(factors, axis=1), ((0, 0), (0, 128 - len(factors))))
        gate_core, up_core = other_core(gate), other_core(up)
        width = share_width // 2
        by_device = w_down[0].reshape(-1, col_count, share_width)
        down_a, down_b = [
            by_device[:, :, begin : begin + width].reshape(-1, col_count * width)
            for begin in (0, width)
        ]
        near = to(down_a, first)
        summed, factors, gate_near, up_near, near, gate_core, up_core, down_a, down_b = ordered(
            summed, factors, gate_near, up_near, near, gate_core, up_core, down_a, down_b
        )
    hidden_mid = (residual.astype(jnp.float32) + summed.astype(jnp.float32)).astype(jnp.bfloat16)
    full_mid = lax.all_gather(hidden_mid, "col", axis=1, tiled=True)
    if dense:
        gate_near, up_near, gate_again, up_again = ordered(gate_near, up_near, gate, up)
        gate_far, up_far = to(gate_again, second), to(up_again, second)
        near_cores = [other_core(value) for value in (gate_near, up_near)]
        gate_far, gate_near, up_near = ordered(gate_far, gate_near, up_near)
        gate_far_2, up_far_2 = to(gate_near, second), to(up_near, second)
        far_cores = [other_core(value) for value in (gate_far, up_far)]
        full_mid, *cores = ordered(full_mid, *near_cores, *far_cores)
        normed = rms_norm(full_mid, gain_post)

        def sets_of(gates, ups, at):
            return inner_of(normed, factors, gates, ups, at)

        inners = sets_of(
            [gate, gate_core, gate_near, cores[0], gate_far, cores[2]],
            [up, up_core, up_near, cores[1], up_far, cores[3]],
            0,
        )
        inners[5], gate_far_2, down_a, near = ordered(inners[5], gate_far_2, down_a, near)
        far, last = to(down_a, second), to(near, second)
        inners += sets_of(
            [gate_far_2, other_core(gate_far_2)], [up_far_2, other_core(up_far_2)], 6
        )
        inners[7], far, down_b = ordered(inners[7], far, down_b)
        downs = both_cores(down_a, near, far, last)
        near, far = to(down_b, first), to(down_b, second)
        total, top = down_sum(inners, downs, None, dec_count)
        tops = [top]
        moe_parts = [lax.psum_scatter(total, "col", scatter_dimension=1, tiled=True)]
        tops[0], near = ordered(tops[0], near)
        last = to(near, second)
        partial = down_sum(inners[:6], both_cores(down_b, near, far))
        partial, last = ordered(partial, last)
        total, top = down_sum(inners[6:], both_cores(last), partial, dec_count)
        top, moe_parts[0] = ordered(top, moe_parts[0])
        tops.append(top)
        moe_parts.append(lax.psum_scatter(total, "col", scatter_dimension=1, tiled=True))
        moe_share = jnp.concatenate(moe_parts, axis=1).astype(jnp.float32)
        hidden_out = (hidden_mid.astype(jnp.float32) + moe_share).astype(jnp.bfloat16)
        full_out = lax.all_gather(hidden_out, "col", axis=1, tiled=True)
        top = jnp.concatenate([top.reshape(dec_count, col_count, width) for top in tops], axis=2)
        top = top.reshape(dec_count, model_width)
        dec_hidden = full_mid[:dec_count].astype(jnp.float32) + shared_sum(top.astype(jnp.bfloat16), "col")
        dec_in = rms_norm(dec_hidden.astype(jnp.bfloat16), gain_input)
    else:
        normed = rms_norm(full_mid, gain_post)
        partial_moe = experts_sent(
            normed, routes, route_weight, w_gate, w_up, w_down, col_count
        )
        moe_share = lax.psum_scatter(partial_moe, "col", scatter_dimension=1, tiled=True)
        hidden_out = (hidden_mid.astype(jnp.float32) + moe_share).astype(jnp.bfloat16)
        full_out = lax.all_gather(hidden_out, "col", axis=1, tiled=True)
        x_in = rms_norm(full_out, gain_input)
        dec_in = x_in[:dec_count]
    dec_rot = rotate(project(dec_in, w_query).reshape(dec_count, heads_local, HD), dec_tables)
    lengths = jnp.stack([cache_lengths // 256, cache_lengths % 256], axis=1).astype(jnp.bfloat16)
    dec_query = jnp.concatenate(
        [
            dec_rot.reshape(dec_count, heads_local * HD),
            jnp.pad(lengths, ((0, 0), (0, HD - lengths.shape[1]))),
        ],
        axis=1,
    )
    outbox = jnp.sum(
        boxes[..., None] * dec_query.astype(jnp.float32)[None, None], axis=2
    ).astype(jnp.bfloat16)
    inbox = lax.all_to_all(outbox, "row", split_axis=0, concat_axis=0, tiled=True)
    slot_terms = jnp.sum(inbox.astype(jnp.float32), axis=0).astype(jnp.bfloat16)
    if dense:
        slot_terms, hidden_out = ordered(slot_terms, hidden_out)
    slot_terms = gathered(slot_terms, "col")
    slot_length = slot_terms[0, :, heads_local * HD :][:, :2].astype(jnp.int32)
    slot_length = slot_length[:, 0] * 256 + slot_length[:, 1]
    slot_query = slot_terms[..., : heads_local * HD]
    slot_query = jnp.moveaxis(slot_query, 0, 1).reshape(dec_count, QH * HD)

    if dense:
        dec_keyval = project(dec_in, w_keyval)
        dec_keys = rotate(dec_keyval[:, None, :HD], dec_tables)[:, 0]
        dec_values = dec_keyval[:, HD:]
    else:
        query_rot = rotate(project(x_in, w_query).reshape(tok_rows, heads_local, HD), tables)
        keyval_local = project(x_in, w_keyval)
        keyval_all = lax.all_gather(keyval_local, "col", axis=1, tiled=True)
        keyval_heads = keyval_all.reshape(tok_rows, KVH, 2, HD)
        key_rot = rotate(keyval_heads[:, :, 0, :], tables)
        value_rows = keyval_heads[:, :, 1, :]
        cache_full = jnp.stack([key_rot, value_rows], axis=2).reshape(tok_rows, 2 * KVH * HD)
        cache_share = cache_full.shape[1] // col_count
        new_cache = lax.dynamic_slice_in_dim(cache_full, col_index * cache_share, cache_share, 1)
        head_kv = col_index * heads_local // (QH // KVH)
        my_keys = lax.dynamic_index_in_dim(key_rot, head_kv, 1, keepdims=False)
        my_values = lax.dynamic_index_in_dim(value_rows, head_kv, 1, keepdims=False)
        dec_keys, dec_values = my_keys[:dec_count], my_values[:dec_count]
        prompt_out = prompt_attention(
            query_rot[dec_count:], my_keys[dec_count:], my_values[dec_count:], segment_ids[0]
        )

    span_len = cache_keys.shape[1]
    span_start = col_index * span_len
    grouped = slot_query.reshape(dec_count, KVH, QH // KVH, HD)
    held_keys = cache_keys.reshape(dec_count, span_len, KVH, HD)
    held_values = cache_values.reshape(dec_count, span_len, KVH, HD).astype(jnp.float32)
    held_scores = (
        jnp.einsum("sgqd,stgd->sgqt", grouped, held_keys, preferred_element_type=jnp.float32)
        * score_scale
    )
    valid = ((span_start + jnp.arange(span_len))[None, :] < slot_length[:, None])[:, None, None, :]
    held_scores = jnp.where(valid, held_scores, NEGATIVE)
    score_top = jnp.max(held_scores, axis=-1)
    held_exp = jnp.where(valid, jnp.exp(held_scores - score_top[..., None]), 0.0)
    weight_mass = jnp.sum(held_exp, axis=-1)
    accum_out = jnp.einsum(
        "sgqt,stgd->sgqd", held_exp, held_values, precision=lax.Precision.HIGHEST
    )

    def packed(accum, top, mass):
        notes = jnp.concatenate([top, mass], axis=-1)
        notes = jnp.pad(notes, ((0, 0),) * (notes.ndim - 1) + ((0, HD - notes.shape[-1]),))
        rows = accum.reshape(accum.shape[:-3] + (dec_count * heads_local, HD))
        return jnp.concatenate([rows, notes], axis=-2)

    def unpacked(rows):
        accum = rows[..., : dec_count * heads_local, :]
        accum = accum.reshape(rows.shape[:-2] + (dec_count, heads_local, HD))
        notes = rows[..., dec_count * heads_local :, :]
        return accum, notes[..., :heads_local], notes[..., heads_local : 2 * heads_local]

    def by_col(value):
        value = value.reshape((dec_count, col_count, heads_local) + value.shape[3:])
        return jnp.moveaxis(value, 1, 0)

    spread_terms = spread(
        packed(by_col(accum_out), by_col(score_top), by_col(weight_mass)), "col"
    )
    accums, tops, masses = unpacked(spread_terms)
    part_top = jnp.max(tops, axis=0)
    scale_by = jnp.exp(tops - part_top[None])
    part_mass = jnp.sum(masses * scale_by, axis=0)
    part_accum = jnp.sum(accums * scale_by[..., None], axis=0)
    reply = packed(part_accum, part_top, part_mass)
    back = lax.all_to_all(
        jnp.broadcast_to(reply[None], (row_count,) + reply.shape),
        "row",
        split_axis=0,
        concat_axis=0,
        tiled=True,
    )
    accums, tops, masses = unpacked(back)

    def picked(value):
        mine = boxes.reshape(boxes.shape + (1,) * (value.ndim - 2))
        return jnp.sum(mine * value[:, :, None], axis=(0, 1))

    remote_top, remote_mass, remote_accum = picked(tops), picked(masses), picked(accums)
    own_query = dec_rot.astype(jnp.float32)
    own_key = dec_keys.astype(jnp.float32)
    own_value = dec_values.astype(jnp.float32)
    own_score = jnp.sum(own_query * own_key[:, None, :], axis=-1) * score_scale
    final_top = jnp.maximum(remote_top, own_score)
    remote_factor = jnp.exp(remote_top - final_top)
    own_factor = jnp.exp(own_score - final_top)
    numerator = (
        remote_accum * remote_factor[..., None] + own_factor[..., None] * own_value[:, None, :]
    )
    denominator = remote_mass * remote_factor + own_factor
    decode_out = (
        (numerator / denominator[..., None])
        .reshape(dec_count, heads_local * HD)
        .astype(jnp.bfloat16)
    )
    if dense:
        segments = jnp.concatenate([jnp.full((dec_count,), -1, jnp.int32), segment_ids[0]])
        window = segment_ids.shape[1] // 2
        new_cache, attention_out = tail(
            full_out,
            gain_input,
            w_query,
            w_keyval,
            tables[0],
            tables[1],
            segments,
            window,
        )
        attention_out = lax.dynamic_update_slice_in_dim(attention_out, decode_out, 0, 0)
        return (hidden_out, new_cache, attention_out)
    attention_out = jnp.concatenate([decode_out, prompt_out], axis=0)
    return (hidden_out, new_cache, attention_out)


def solution(mesh):
    return jax.shard_map(
        shards,
        mesh=mesh,
        in_specs=(
            P("row", "col"),
            P("row", "col"),
            P("col", None),
            P(),
            P(),
            P("row", None),
            P("row", None),
            P(("row", "col"), None, None),
            P(("row", "col"), None, None),
            P(("row", "col"), None, None),
            P(None, "col"),
            P(None, "col"),
            P("row", None),
            P("row"),
            P("row"),
            P("row", "col", None),
            P("row", "col", None),
        ),
        out_specs=(P("row", "col"), P("row", "col"), P("row", "col")),
        check_vma=False,
    )
```

```python
import jax
import jax.numpy as jnp
from jax import lax
from jax.experimental import pallas as pl
from jax.experimental.pallas import tpu as pltpu
from jax.sharding import PartitionSpec as P

TOP = 8
QH = 32
KVH = 4
HD = 128


EPSILON = 1e-06
ROPE_THETA = 1000000.0
NEGATIVE = -1e30
VMEM_BYTES = 60 * 1024 * 1024


def rms_norm(hidden, gain_vector):
    values = hidden.astype(jnp.float32)
    inverse = lax.rsqrt(jnp.mean(values * values, axis=-1, keepdims=True) + EPSILON)
    return (values * inverse * gain_vector.astype(jnp.float32)).astype(jnp.bfloat16)


def rotary_tables(positions):
    half_width = HD // 2
    indices = jnp.arange(half_width).astype(jnp.float32)
    inverse = ROPE_THETA ** (-2.0 * indices / HD)
    angles = positions.astype(jnp.float32)[:, None] * inverse[None, :]
    cosine, sine_part = jnp.cos(angles), jnp.sin(angles)
    return (
        jnp.concatenate([cosine, cosine], axis=-1),
        jnp.concatenate([-sine_part, sine_part], axis=-1),
    )


def rotate(values, tables):
    cosine, sine_part = (table[:, None, :] for table in tables)
    half_width = HD // 2
    floats = values.astype(jnp.float32)
    turned = jnp.concatenate([floats[..., half_width:], floats[..., :half_width]], axis=-1)
    return (floats * cosine + turned * sine_part).astype(jnp.bfloat16)


def segment_positions(segment_rows):
    earlier = jnp.sum((segment_rows[None, :] < segment_rows[:, None]).astype(jnp.int32), axis=1)
    return jnp.arange(segment_rows.shape[0], dtype=jnp.int32) - earlier


def shifted(block, axis, count, shift):
    return lax.ppermute(block, axis, [(i, (i + shift) % count) for i in range(count)])


def shifted(value, axis, shift):
    count = lax.axis_size(axis)
    return lax.ppermute(value, axis, [(i, (i + shift) % count) for i in range(count)])


def spread(blocks, axis):
    count = lax.axis_size(axis)
    index = lax.axis_index(axis)
    mine = [
        lax.dynamic_index_in_dim(blocks, (index + shift) % count, 0, keepdims=False)
        for shift in range(count)
    ]
    return jnp.stack([mine[0]] + [shifted(mine[k], axis, k) for k in range(1, count)])


def gathered(block, axis):
    count = lax.axis_size(axis)
    index = lax.axis_index(axis)
    arrived = [block] + [shifted(block, axis, k) for k in range(1, count)]
    order = jnp.stack(arrived + arrived)
    return jnp.stack(
        [
            lax.dynamic_index_in_dim(order, index - i + count, 0, keepdims=False)
            for i in range(count)
        ]
    )


def shared_sum(block, axis):
    count = lax.axis_size(axis)
    total = block.astype(jnp.float32)
    for k in range(1, count):
        total = total + shifted(block, axis, k).astype(jnp.float32)
    return total


def inner_kernel(sets, at, x_ref, factor_ref, *refs):
    outs = refs[2 * sets :]
    tile = outs[0].shape[1]
    for pair in range(0, sets, 2):
        weights = jnp.concatenate([ref[...] for ref in refs[2 * pair : 2 * pair + 4]], axis=1)
        products = jnp.dot(x_ref[...], weights, preferred_element_type=jnp.float32)
        for which in range(2):
            gate = products[:, 2 * which * tile : (2 * which + 1) * tile]
            up = products[:, (2 * which + 1) * tile : (2 * which + 2) * tile]
            place = at + pair + which
            inner = jax.nn.silu(gate) * up * factor_ref[:, place : place + 1]
            outs[pair + which][...] = inner.astype(jnp.bfloat16)


def inner_of(normed, factors, gates, ups, at):
    tok_rows, model_width = normed.shape
    half = gates[0].shape[1]
    tile = 128
    sets = len(gates)
    moving = pl.BlockSpec((model_width, tile), lambda step: (0, step))

    def fixed(shape):
        return pl.BlockSpec(shape, lambda step: (0, 0))

    return list(
        pl.pallas_call(
            lambda *refs: inner_kernel(sets, at, *refs),
            grid=(half // tile,),
            out_shape=[jax.ShapeDtypeStruct((tok_rows, half), jnp.bfloat16)] * sets,
            in_specs=[fixed(normed.shape), fixed(factors.shape)] + [moving] * 2 * sets,
            out_specs=[pl.BlockSpec((tok_rows, tile), lambda step: (0, step))] * sets,
            compiler_params=pltpu.CompilerParams(vmem_limit_bytes=VMEM_BYTES),
            cost_estimate=pl.CostEstimate(
                flops=tok_rows, bytes_accessed=tok_rows, transcendentals=0
            ),
        )(normed, factors, *[value for both in zip(gates, ups) for value in both])
    )


def down_kernel(sets, *refs):
    inners, downs = refs[:sets], refs[sets : 2 * sets]
    acc = None
    for pair in range(0, sets, 2):
        left = jnp.concatenate([inners[pair][...], inners[pair + 1][...]], axis=1)
        right = jnp.concatenate([downs[pair][...], downs[pair + 1][...]], axis=0)
        product = jnp.dot(left, right, preferred_element_type=jnp.float32)
        acc = product if acc is None else acc + product
    if len(refs) == 2 * sets + 1:
        refs[-1][...] = acc
    else:
        total_ref, top_ref = refs[-2:]
        if len(refs) == 2 * sets + 3:
            acc = acc + refs[2 * sets][...]
        total_ref[...] = acc.astype(jnp.bfloat16)
        top_ref[...] = acc[0 : top_ref.shape[0], :]


def down_sum(inners, downs, before=None, tops=0):
    sets = len(inners)
    tok_rows, half = inners[0].shape
    width = downs[0].shape[1]
    tile = 256

    def moving(rows):
        return pl.BlockSpec((rows, tile), lambda step: (0, step))

    whole = jax.ShapeDtypeStruct((tok_rows, width), jnp.float32)
    rounded = [
        jax.ShapeDtypeStruct((tok_rows, width), jnp.bfloat16),
        jax.ShapeDtypeStruct((tops, width), jnp.float32),
    ]
    last, more = tops > 0, before is not None
    return pl.pallas_call(
        lambda *refs: down_kernel(sets, *refs),
        grid=(width // tile,),
        out_shape=rounded if last else whole,
        in_specs=[pl.BlockSpec((tok_rows, half), lambda step: (0, 0))] * sets
        + [moving(half)] * sets
        + [moving(tok_rows)] * more,
        out_specs=[moving(tok_rows), moving(tops)] if last else moving(tok_rows),
        compiler_params=pltpu.CompilerParams(vmem_limit_bytes=VMEM_BYTES),
        cost_estimate=pl.CostEstimate(
            flops=2 * tok_rows * width * sets * half,
            bytes_accessed=2 * sets * half * (width + tok_rows) + 4 * tok_rows * width,
            transcendentals=0,
        ),
    )(*inners, *downs, *([before] if more else []))


def tail_kernel(window, *refs):
    (full, gain, wq, wkv, cosine, sine, seg_col, seg_row, cache_ref, out_ref) = refs[:10]
    x_in, keys, values, bias = refs[10:]
    tok_rows = x_in.shape[0]
    rows = 128

    def turn(block):
        floats = block.astype(jnp.float32)
        turned = pltpu.roll(floats, HD // 2, 1)
        return (floats * cosine[...] + turned * sine[...]).astype(jnp.bfloat16)

    @pl.when(pl.program_id(0) == 0)
    def _():
        for start in range(0, tok_rows, rows):
            place = slice(start, start + rows)
            floats = full[place, :].astype(jnp.float32)
            inverse = lax.rsqrt(jnp.mean(floats * floats, axis=-1, keepdims=True) + EPSILON)
            x_in[place, :] = (floats * inverse * gain[...].astype(jnp.float32)).astype(jnp.bfloat16)
        keyval = jnp.dot(x_in[...], wkv[...], preferred_element_type=jnp.float32)
        keyval = keyval.astype(jnp.bfloat16)
        keys[...] = turn(keyval[:, :HD])
        values[...] = keyval[:, HD:]
        cache_ref[:, :HD] = keys[...]
        cache_ref[:, HD:] = values[...]
        ordinal = lax.broadcasted_iota(jnp.int32, (tok_rows, tok_rows), 0)
        other = lax.broadcasted_iota(jnp.int32, (tok_rows, tok_rows), 1)
        allowed = (seg_col[...] == seg_row[...]) & (other <= ordinal)
        bias[...] = jnp.where(allowed, 0.0, NEGATIVE)

    queries = jnp.dot(x_in[...], wq[...], preferred_element_type=jnp.float32).astype(jnp.bfloat16)
    heads = wq.shape[1] // HD
    turned = [turn(queries[:, head * HD : (head + 1) * HD]) for head in range(heads)]
    step = 128
    for start in range(0, tok_rows, step):
        first = max(0, (start - window + 1) // step * step)
        stop = start + step
        query = jnp.concatenate([head[start:stop] for head in turned], axis=0)
        scores = lax.dot_general(
            query,
            keys[first:stop, :],
            (((1,), (1,)), ((), ())),
            preferred_element_type=jnp.float32,
        ) * HD ** (-0.5)
        scores = scores.reshape(heads, step, stop - first) + bias[start:stop, first:stop][None]
        scores = scores.reshape(heads * step, stop - first)
        highest = jnp.max(scores, axis=-1, keepdims=True)
        exponent = jnp.exp(scores - highest)
        mass = jnp.sum(exponent, axis=-1, keepdims=True)
        mixed = jnp.dot(
            exponent.astype(jnp.bfloat16), values[first:stop, :], preferred_element_type=jnp.float32
        )
        mixed = (mixed * (1.0 / mass)).astype(jnp.bfloat16)
        for head in range(heads):
            out_ref[start:stop, head * HD : (head + 1) * HD] = mixed[head * step : (head + 1) * step]


def tail(full, gain, w_query, w_keyval, cosine, sine, segments, window):
    tok_rows = segments.shape[0]
    model_width = w_query.shape[0]
    query_width = w_query.shape[1]
    pair, some = 2 * HD, min(4 * HD, query_width)

    def fixed(shape):
        return pl.BlockSpec(shape, lambda step: (0, 0))

    def moving(shape):
        return pl.BlockSpec(shape, lambda step: (0, step))

    return pl.pallas_call(
        lambda *refs: tail_kernel(window, *refs),
        grid=(query_width // some,),
        out_shape=[
            jax.ShapeDtypeStruct((tok_rows, pair), jnp.bfloat16),
            jax.ShapeDtypeStruct((tok_rows, query_width), jnp.bfloat16),
        ],
        in_specs=[
            fixed(full.shape),
            fixed((1, model_width)),
            moving((model_width, some)),
            fixed((model_width, pair)),
            fixed((tok_rows, HD)),
            fixed((tok_rows, HD)),
            fixed((tok_rows, 1)),
            fixed((1, tok_rows)),
        ],
        out_specs=[fixed((tok_rows, pair)), moving((tok_rows, some))],
        scratch_shapes=[
            pltpu.VMEM((tok_rows, model_width), jnp.bfloat16),
            pltpu.VMEM((tok_rows, HD), jnp.bfloat16),
            pltpu.VMEM((tok_rows, HD), jnp.bfloat16),
            pltpu.VMEM((tok_rows, tok_rows), jnp.float32),
        ],
        compiler_params=pltpu.CompilerParams(vmem_limit_bytes=VMEM_BYTES),
        cost_estimate=pl.CostEstimate(
            flops=2 * tok_rows * model_width * (query_width + pair),
            bytes_accessed=2 * model_width * (query_width + pair + 2 * tok_rows),
            transcendentals=tok_rows * tok_rows * query_width // HD,
        ),
    )(
        full,
        gain[None],
        w_query,
        w_keyval,
        cosine,
        sine,
        segments[:, None],
        segments[None],
    )


def ordered(*values):
    return lax.optimization_barrier(values)


def row_pairs():
    first = [(r, r ^ (4 if r & 1 else 2)) for r in range(8)]
    second = [(r, r ^ (2 if r & 1 else 4)) for r in range(8)]
    core = [(r, r ^ 1) for r in range(8)]
    return first, second, core


def other_core(value):
    return lax.ppermute(value, "row", row_pairs()[2])


def both_cores(*values):
    return [copy for value in values for copy in (value, other_core(value))]


def row_sources():
    row = lax.axis_index("row")
    one = jnp.where(row % 2 == 0, 2, 4)
    other = 6 - one
    flips = [0, 1, one, 1 + other, other, 1 + one, 6, 7]
    return [row ^ flip for flip in flips]


def expert_of(source, col_count):
    return (source * col_count + lax.axis_index("col")) // 2


def naming(routes, route_weight, expert):
    return jnp.sum(jnp.where(routes == expert, route_weight, 0.0), axis=1, keepdims=True)


def experts_sent(normed, routes, route_weight, w_gate, w_up, w_down, col_count):
    col_index = lax.axis_index("col")
    row_count = lax.axis_size("row")
    tok_rows, model_width = normed.shape
    group_width = col_count // 2
    capacity = 2 * tok_rows * TOP // (row_count * group_width)
    matching = routes % group_width == col_index // 2
    target = routes // group_width
    dest_ids = jnp.arange(row_count, dtype=jnp.int32)
    hitting = matching[:, :, None] & (target[:, :, None] == dest_ids[None, None, :])
    sent_flag = jnp.sum(hitting.astype(jnp.int32), axis=1)
    sent_weight = jnp.sum(jnp.where(hitting, route_weight[:, :, None], 0.0), axis=1)
    place = jnp.cumsum(sent_flag, axis=0) - sent_flag
    dest_or_drop = jnp.where(sent_flag > 0, dest_ids[None, :], row_count)
    row_ids = jnp.broadcast_to(
        jnp.arange(tok_rows, dtype=jnp.int32)[:, None], (tok_rows, row_count)
    )
    slot_rows = (
        jnp.full((row_count, capacity), tok_rows, jnp.int32)
        .at[dest_or_drop, place]
        .set(row_ids, mode="drop")
    )
    slot_weight = (
        jnp.zeros((row_count, capacity), jnp.float32)
        .at[dest_or_drop, place]
        .set(sent_weight, mode="drop")
    )
    padded = jnp.concatenate([normed, jnp.zeros((1, model_width), jnp.bfloat16)], axis=0)
    outgoing = padded[slot_rows]
    arrived = lax.all_to_all(outgoing, "row", split_axis=0, concat_axis=0, tiled=True)
    flat_rows = arrived.reshape(-1, arrived.shape[2])
    gate_part = jnp.dot(flat_rows, w_gate[0], preferred_element_type=jnp.float32)
    up_part = jnp.dot(flat_rows, w_up[0], preferred_element_type=jnp.float32)
    inner = (jax.nn.silu(gate_part) * up_part).astype(jnp.bfloat16)
    result = jnp.dot(inner, w_down[0], preferred_element_type=jnp.float32).astype(jnp.bfloat16)
    returned = lax.all_to_all(
        result.reshape(arrived.shape), "row", split_axis=0, concat_axis=0, tiled=True
    )
    weighted = slot_weight[:, :, None] * returned.astype(jnp.float32)
    return (
        jnp.zeros((tok_rows, model_width), jnp.float32)
        .at[slot_rows.reshape(-1)]
        .add(weighted.reshape(-1, model_width), mode="drop")
    )


def prompt_attention(prompt_query, prompt_keys, prompt_values, segment_rows):
    prompt_rows = prompt_query.shape[0]
    scores = jnp.einsum(
        "ihd,jd->hij", prompt_query, prompt_keys, preferred_element_type=jnp.float32
    ) * HD ** (-0.5)
    ordinal = jnp.arange(prompt_rows)
    allowed = (segment_rows[:, None] == segment_rows[None, :]) & (
        ordinal[None, :] <= ordinal[:, None]
    )
    scores = jnp.where(allowed[None, :, :], scores, NEGATIVE)
    highest = jnp.max(scores, axis=-1, keepdims=True)
    exponent = jnp.exp(scores - highest)
    probability = (exponent / jnp.sum(exponent, axis=-1, keepdims=True)).astype(jnp.bfloat16)
    prompt_out = jnp.einsum(
        "hij,jd->ihd", probability, prompt_values, preferred_element_type=jnp.float32
    )
    return prompt_out.astype(jnp.bfloat16).reshape(prompt_rows, -1)


def shards(
    attn_context,
    residual,
    w_out,
    gain_post,
    gain_input,
    routes,
    router_scores,
    w_gate,
    w_up,
    w_down,
    w_query,
    w_keyval,
    segment_ids,
    cache_lengths,
    holders,
    cache_keys,
    cache_values,
):
    col_index = lax.axis_index("col")
    col_count = lax.axis_size("col")
    row_count = lax.axis_size("row")
    tok_rows = attn_context.shape[0]
    share_width = residual.shape[1]
    model_width = share_width * col_count
    dec_count = cache_lengths.shape[0]
    expert_count = row_count * col_count // 2
    dense = row_count == 8 and expert_count <= 2 * TOP and col_count == KVH

    holder_dev = holders // dec_count
    holder_slot = holders % dec_count
    heads_local = QH // col_count
    score_scale = HD ** (-0.5)
    prompt_pos = segment_positions(segment_ids[0])
    tables = rotary_tables(jnp.concatenate([cache_lengths, prompt_pos], axis=0))
    dec_tables = [table[:dec_count] for table in tables]

    def project(rows, weights):
        return jnp.dot(rows, weights, preferred_element_type=jnp.float32).astype(jnp.bfloat16)

    boxes = (
        (holder_dev[None, None, :] == jnp.arange(row_count)[:, None, None])
        & (holder_slot[None, None, :] == jnp.arange(dec_count)[None, :, None])
    ).astype(jnp.float32)
    route_weight = router_scores / jnp.sum(router_scores, axis=1, keepdims=True)

    if dense:
        gate, up = w_gate[0], w_up[0]
    projected = jnp.dot(attn_context, w_out, preferred_element_type=jnp.float32)
    summed = lax.psum_scatter(
        projected.astype(jnp.bfloat16), "col", scatter_dimension=1, tiled=True
    )
    if dense:
        first, second, _ = row_pairs()

        def to(value, pairs):
            return lax.ppermute(value, "row", pairs)

        gate_near, up_near = to(gate, first), to(up, first)
        experts = [expert_of(source, col_count) for source in row_sources()]
        factors = [naming(routes, route_weight, expert) for expert in experts]
        factors = jnp.pad(jnp.concatenate(factors, axis=1), ((0, 0), (0, 128 - len(factors))))
        gate_core, up_core = other_core(gate), other_core(up)
        width = share_width // 2
        by_device = w_down[0].reshape(-1, col_count, share_width)
        down_a, down_b = [
            by_device[:, :, begin : begin + width].reshape(-1, col_count * width)
            for begin in (0, width)
        ]
        near = to(down_a, first)
        summed, factors, gate_near, up_near, near, gate_core, up_core, down_a, down_b = ordered(
            summed, factors, gate_near, up_near, near, gate_core, up_core, down_a, down_b
        )
    hidden_mid = (residual.astype(jnp.float32) + summed.astype(jnp.float32)).astype(jnp.bfloat16)
    full_mid = lax.all_gather(hidden_mid, "col", axis=1, tiled=True)
    if dense:
        gate_near, up_near, gate_again, up_again = ordered(gate_near, up_near, gate, up)
        gate_far, up_far = to(gate_again, second), to(up_again, second)
        near_cores = [other_core(value) for value in (gate_near, up_near)]
        gate_far_2, up_far_2 = to(gate_near, second), to(up_near, second)
        full_mid, gate_far, up_far, gate_far_2, *cores = ordered(
            full_mid, gate_far, up_far, gate_far_2, *near_cores
        )
        normed = rms_norm(full_mid, gain_post)

        def sets_of(gates, ups, at):
            return inner_of(normed, factors, gates, ups, at)

        inners = sets_of(
            [gate, gate_core, gate_near, cores[0]], [up, up_core, up_near, cores[1]], 0
        )
        inners[3], up_far_2, down_a, near = ordered(inners[3], up_far_2, down_a, near)
        far, last = to(down_a, second), to(near, second)
        inners += sets_of(both_cores(gate_far, gate_far_2), both_cores(up_far, up_far_2), 4)
        inners[7], far, last, down_b = ordered(inners[7], far, last, down_b)
        downs = both_cores(down_a, near, far, last)
        near, far = to(down_b, first), to(down_b, second)
        total, top = down_sum(inners, downs, None, dec_count)
        tops = [top]
        moe_parts = [lax.psum_scatter(total, "col", scatter_dimension=1, tiled=True)]
        tops[0], near = ordered(tops[0], near)
        last = to(near, second)
        partial = down_sum(inners[:6], both_cores(down_b, near, far))
        partial, last = ordered(partial, last)
        total, top = down_sum(inners[6:], both_cores(last), partial, dec_count)
        top, moe_parts[0] = ordered(top, moe_parts[0])
        tops.append(top)
        moe_parts.append(lax.psum_scatter(total, "col", scatter_dimension=1, tiled=True))
        moe_share = jnp.concatenate(moe_parts, axis=1).astype(jnp.float32)
        hidden_out = (hidden_mid.astype(jnp.float32) + moe_share).astype(jnp.bfloat16)
        full_out = lax.all_gather(hidden_out, "col", axis=1, tiled=True)
        top = jnp.concatenate([top.reshape(dec_count, col_count, width) for top in tops], axis=2)
        top = top.reshape(dec_count, model_width)
        dec_hidden = full_mid[:dec_count].astype(jnp.float32) + shared_sum(top.astype(jnp.bfloat16), "col")
        dec_in = rms_norm(dec_hidden.astype(jnp.bfloat16), gain_input)
    else:
        normed = rms_norm(full_mid, gain_post)
        partial_moe = experts_sent(
            normed, routes, route_weight, w_gate, w_up, w_down, col_count
        )
        moe_share = lax.psum_scatter(partial_moe, "col", scatter_dimension=1, tiled=True)
        hidden_out = (hidden_mid.astype(jnp.float32) + moe_share).astype(jnp.bfloat16)
        full_out = lax.all_gather(hidden_out, "col", axis=1, tiled=True)
        x_in = rms_norm(full_out, gain_input)
        dec_in = x_in[:dec_count]
    dec_rot = rotate(project(dec_in, w_query).reshape(dec_count, heads_local, HD), dec_tables)
    lengths = jnp.stack([cache_lengths // 256, cache_lengths % 256], axis=1).astype(jnp.bfloat16)
    dec_query = jnp.concatenate(
        [
            dec_rot.reshape(dec_count, heads_local * HD),
            jnp.pad(lengths, ((0, 0), (0, HD - lengths.shape[1]))),
        ],
        axis=1,
    )
    outbox = jnp.sum(
        boxes[..., None] * dec_query.astype(jnp.float32)[None, None], axis=2
    ).astype(jnp.bfloat16)
    inbox = lax.all_to_all(outbox, "row", split_axis=0, concat_axis=0, tiled=True)
    slot_terms = jnp.sum(inbox.astype(jnp.float32), axis=0).astype(jnp.bfloat16)
    if dense:
        slot_terms, hidden_out = ordered(slot_terms, hidden_out)
    slot_terms = gathered(slot_terms, "col")
    slot_length = slot_terms[0, :, heads_local * HD :][:, :2].astype(jnp.int32)
    slot_length = slot_length[:, 0] * 256 + slot_length[:, 1]
    slot_query = slot_terms[..., : heads_local * HD]
    slot_query = jnp.moveaxis(slot_query, 0, 1).reshape(dec_count, QH * HD)

    if dense:
        dec_keyval = project(dec_in, w_keyval)
        dec_keys = rotate(dec_keyval[:, None, :HD], dec_tables)[:, 0]
        dec_values = dec_keyval[:, HD:]
    else:
        query_rot = rotate(project(x_in, w_query).reshape(tok_rows, heads_local, HD), tables)
        keyval_local = project(x_in, w_keyval)
        keyval_all = lax.all_gather(keyval_local, "col", axis=1, tiled=True)
        keyval_heads = keyval_all.reshape(tok_rows, KVH, 2, HD)
        key_rot = rotate(keyval_heads[:, :, 0, :], tables)
        value_rows = keyval_heads[:, :, 1, :]
        cache_full = jnp.stack([key_rot, value_rows], axis=2).reshape(tok_rows, 2 * KVH * HD)
        cache_share = cache_full.shape[1] // col_count
        new_cache = lax.dynamic_slice_in_dim(cache_full, col_index * cache_share, cache_share, 1)
        head_kv = col_index * heads_local // (QH // KVH)
        my_keys = lax.dynamic_index_in_dim(key_rot, head_kv, 1, keepdims=False)
        my_values = lax.dynamic_index_in_dim(value_rows, head_kv, 1, keepdims=False)
        dec_keys, dec_values = my_keys[:dec_count], my_values[:dec_count]
        prompt_out = prompt_attention(
            query_rot[dec_count:], my_keys[dec_count:], my_values[dec_count:], segment_ids[0]
        )

    span_len = cache_keys.shape[1]
    span_start = col_index * span_len
    grouped = slot_query.reshape(dec_count, KVH, QH // KVH, HD)
    held_keys = cache_keys.reshape(dec_count, span_len, KVH, HD)
    held_values = cache_values.reshape(dec_count, span_len, KVH, HD).astype(jnp.float32)
    held_scores = (
        jnp.einsum("sgqd,stgd->sgqt", grouped, held_keys, preferred_element_type=jnp.float32)
        * score_scale
    )
    valid = ((span_start + jnp.arange(span_len))[None, :] < slot_length[:, None])[:, None, None, :]
    held_scores = jnp.where(valid, held_scores, NEGATIVE)
    score_top = jnp.max(held_scores, axis=-1)
    held_exp = jnp.where(valid, jnp.exp(held_scores - score_top[..., None]), 0.0)
    weight_mass = jnp.sum(held_exp, axis=-1)
    accum_out = jnp.einsum(
        "sgqt,stgd->sgqd", held_exp, held_values, precision=lax.Precision.HIGHEST
    )

    def packed(accum, top, mass):
        notes = jnp.concatenate([top, mass], axis=-1)
        notes = jnp.pad(notes, ((0, 0),) * (notes.ndim - 1) + ((0, HD - notes.shape[-1]),))
        rows = accum.reshape(accum.shape[:-3] + (dec_count * heads_local, HD))
        return jnp.concatenate([rows, notes], axis=-2)

    def unpacked(rows):
        accum = rows[..., : dec_count * heads_local, :]
        accum = accum.reshape(rows.shape[:-2] + (dec_count, heads_local, HD))
        notes = rows[..., dec_count * heads_local :, :]
        return accum, notes[..., :heads_local], notes[..., heads_local : 2 * heads_local]

    def by_col(value):
        value = value.reshape((dec_count, col_count, heads_local) + value.shape[3:])
        return jnp.moveaxis(value, 1, 0)

    spread_terms = spread(
        packed(by_col(accum_out), by_col(score_top), by_col(weight_mass)), "col"
    )
    accums, tops, masses = unpacked(spread_terms)
    part_top = jnp.max(tops, axis=0)
    scale_by = jnp.exp(tops - part_top[None])
    part_mass = jnp.sum(masses * scale_by, axis=0)
    part_accum = jnp.sum(accums * scale_by[..., None], axis=0)
    reply = packed(part_accum, part_top, part_mass)
    back = lax.all_to_all(
        jnp.broadcast_to(reply[None], (row_count,) + reply.shape),
        "row",
        split_axis=0,
        concat_axis=0,
        tiled=True,
    )
    accums, tops, masses = unpacked(back)

    def picked(value):
        mine = boxes.reshape(boxes.shape + (1,) * (value.ndim - 2))
        return jnp.sum(mine * value[:, :, None], axis=(0, 1))

    remote_top, remote_mass, remote_accum = picked(tops), picked(masses), picked(accums)
    own_query = dec_rot.astype(jnp.float32)
    own_key = dec_keys.astype(jnp.float32)
    own_value = dec_values.astype(jnp.float32)
    own_score = jnp.sum(own_query * own_key[:, None, :], axis=-1) * score_scale
    final_top = jnp.maximum(remote_top, own_score)
    remote_factor = jnp.exp(remote_top - final_top)
    own_factor = jnp.exp(own_score - final_top)
    numerator = (
        remote_accum * remote_factor[..., None] + own_factor[..., None] * own_value[:, None, :]
    )
    denominator = remote_mass * remote_factor + own_factor
    decode_out = (
        (numerator / denominator[..., None])
        .reshape(dec_count, heads_local * HD)
        .astype(jnp.bfloat16)
    )
    if dense:
        segments = jnp.concatenate([jnp.full((dec_count,), -1, jnp.int32), segment_ids[0]])
        window = segment_ids.shape[1] // 2
        new_cache, attention_out = tail(
            full_out,
            gain_input,
            w_query,
            w_keyval,
            tables[0],
            tables[1],
            segments,
            window,
        )
        attention_out = lax.dynamic_update_slice_in_dim(attention_out, decode_out, 0, 0)
        return (hidden_out, new_cache, attention_out)
    attention_out = jnp.concatenate([decode_out, prompt_out], axis=0)
    return (hidden_out, new_cache, attention_out)


def solution(mesh):
    return jax.shard_map(
        shards,
        mesh=mesh,
        in_specs=(
            P("row", "col"),
            P("row", "col"),
            P("col", None),
            P(),
            P(),
            P("row", None),
            P("row", None),
            P(("row", "col"), None, None),
            P(("row", "col"), None, None),
            P(("row", "col"), None, None),
            P(None, "col"),
            P(None, "col"),
            P("row", None),
            P("row"),
            P("row"),
            P("row", "col", None),
            P("row", "col", None),
        ),
        out_specs=(P("row", "col"), P("row", "col"), P("row", "col")),
        check_vma=False,
    )
```
